1024 devices in a mesh: wide: 128 (over y, z), narrow: 8 (over x, core).
Axes of the slice: x: 4, y: 4, z: 32, core: 2. Of those that a mesh axis runs over, the one named last changes fastest.
Arguments:
- features: float32 [262144, 128], P(('wide', 'narrow')), may hold values from -6 to 6
- columns: int32 [4096, 16], P(('wide', 'narrow')), may hold values from 0 to 4095, as said below
- counts: int32 [4096], P(('wide', 'narrow')), may hold values from 1 to 16, as said below
- blocks: float32 [4096, 64, 1024], P(('wide', 'narrow')), may hold values from -0.1875 to 0.1875
- weight: float32 [128, 256], replicated, may hold values from -0.5 to 0.5
- bias: float32 [256], replicated, may hold values from -3 to 3
- cotangent: float32 [262144, 256], P(('wide', 'narrow')), may hold values from -24 to 24
Outputs:
- hidden: float32 [262144, 256], P(('wide', 'narrow'))
- weight_grad: float32 [128, 256], replicated
- bias_grad: float32 [256], replicated
- feature_grad: float32 [262144, 128], P(('wide', 'narrow'))
The draws below stay inside these ranges and needn't reach their ends.
Inputs may be any that keep to these rules, and one draw needn't show every extreme that they name: The block column of any slot of block row r lies in stripes r // 32 - 1 to r // 32 + 1, where stripe t holds block columns t * 32 to (t + 1) * 32 - 1. `counts`: among the 4 block rows of each device one has all 16 slots in use.
All inputs are finite; a program needn't handle non-finite values.
Results may differ from the reference program's by a relative error of at most 0.0003.
Values sent between devices are 32-bit elements; how exact they have to be, the bound alone decides.
No kernel may reach another device: no remote copies, remote signals or barrier semaphores. Data moves between devices by JAX's collectives and lax.ppermute only.
A program may use at most 32 MiB of HBM per device.

```python
import jax
import jax.numpy as jnp
from jax import lax

D_IN = 128
HID = 256
BLK = 64
K = 16
BR = 4
SB = 32
NBR = 4096
NODES = 262144


def draw_columns(key, part):
    key = jax.random.fold_in(key, 12)
    stripe = (jnp.arange(NBR, dtype=jnp.int32) // SB)[:, None]
    offset = jax.random.randint(key, (NBR, K), -SB, 2 * SB, dtype=jnp.int32)
    column = stripe * SB + offset
    column = jnp.where(column < 0, column + SB, column)
    column = jnp.where(column >= NBR, column - SB, column)
    return column.astype(jnp.int32)


def draw_counts(key, part):
    key = jax.random.fold_in(key, 13)
    key_base, key_pos = jax.random.split(key)
    base = jax.random.randint(key_base, (NBR // BR, BR), 1, K + 1, dtype=jnp.int32)
    place = jax.random.randint(key_pos, (NBR // BR, 1), 0, BR, dtype=jnp.int32)
    within = jnp.arange(BR, dtype=jnp.int32)[None, :]
    filled = jnp.where(within == place, K, base)
    return filled.reshape(NBR).astype(jnp.int32)


def with_spikes(drawn, stream_key, source, target, blocks, factor):
    owner, partner = [(jnp.arange(drawn.shape[axis_at]) // (drawn.shape[axis_at] // blocks)).reshape([-1 if axis == axis_at else 1 for axis in range(drawn.ndim)]) for axis_at in (source, target)]
    chosen = jax.random.permutation(stream_key, blocks)[partner]
    strong = (owner == chosen) | (owner == (partner + blocks // 2) % blocks)
    return jnp.where(strong, factor * drawn, drawn)


def steps_of(rng, shape, cuts, least, top_value):
    loudness = 1.0
    for axis_at, parts in cuts:
        heights = jax.random.uniform(jax.random.fold_in(jax.random.fold_in(rng, 6), axis_at), (parts,), jnp.float32, least / len(cuts), top_value / len(cuts))
        loudness = loudness * jnp.repeat(jnp.exp(heights), shape[axis_at] // parts).reshape((-1,) + (1,) * (len(shape) - 1 - axis_at))
    return loudness


def normal_values(rng, extent, deviation, limit, pieces=(), kind=jnp.bfloat16):
    entries = deviation * jax.random.normal(rng, extent, jnp.float32)
    if pieces:
        entries = entries * steps_of(rng, extent, pieces, -0.22, 0.18)
    return jnp.clip(entries, -limit, limit).astype(kind)


def noise_with(key, dims, width, limit, pieces, heavy, kind=jnp.bfloat16):
    array = width * jax.random.normal(key, dims, jnp.float32)
    if pieces:
        array = array * steps_of(key, dims, pieces, -0.22, 0.18)
    return jnp.clip(with_spikes(array, jax.random.fold_in(key, 3), *heavy), -limit, limit).astype(kind)


def setup_inputs(seed: int = 0) -> dict:
    key_of = jax.random.split(jax.random.key(seed), 8)
    features = normal_values(key_of[0], (NODES, D_IN), 1.0, 6.0, ((0, 1024),), jnp.float32)
    columns = draw_columns(jax.random.fold_in(key_of[7], 71), 0)
    counts = draw_counts(jax.random.fold_in(key_of[7], 71), 0)
    blocks = normal_values(key_of[3], (NBR, BLK, K * BLK), (K * BLK) ** -0.5, 0.1875, ((0, 1024),), jnp.float32)
    weight = normal_values(key_of[4], (D_IN, HID), D_IN ** -0.5, 0.5, (), jnp.float32)
    bias = normal_values(key_of[5], (HID,), 0.5, 3.0, (), jnp.float32)
    cotangent = noise_with(key_of[6], (NODES, HID), 1.0, 24.0, ((0, 1024),), (0, 1, 256, 6.0), jnp.float32)
    return dict(features=features, columns=columns, counts=counts, blocks=blocks, weight=weight, bias=bias, cotangent=cotangent)


def activate(value):
    return jax.nn.gelu(value, approximate=True)

def reference(features, columns, counts, blocks, weight, bias, cotangent):
    hi = lax.Precision.HIGHEST
    nbr = columns.shape[0]
    groups = nbr // BR
    feat_blocks = features.reshape(nbr, BLK, D_IN)
    slot_of = (jnp.arange(K * BLK, dtype=jnp.int32) // BLK)[None, :]
    usage = (slot_of < counts[:, None]).astype(jnp.float32)
    masked = blocks * usage[:, None, :]
    col_groups = columns.reshape(groups, BR, K)
    val_groups = masked.reshape(groups, BR, BLK, K * BLK)

    def forward_group(args):
        cols, vals = args
        picked = jnp.take(feat_blocks, cols.reshape(-1), axis=0).reshape(BR, K * BLK, D_IN)
        return jnp.einsum('rim,rmf->rif', vals, picked, precision=hi)
    aggregated = lax.map(forward_group, (col_groups, val_groups)).reshape(NODES, D_IN)
    preact = jnp.dot(aggregated, weight, precision=hi) + bias
    hidden, pullback = jax.vjp(activate, preact)
    dpre = pullback(cotangent)[0]
    weight_grad = jnp.dot(aggregated.T, dpre, precision=hi)
    bias_grad = lax.optimization_barrier(jnp.sum(dpre, axis=0))
    dagg = jnp.dot(dpre, weight.T, precision=hi).reshape(groups, BR, BLK, D_IN)

    def backward_group(total, args):
        cols, vals, grads = args
        terms = jnp.einsum('rim,rif->rmf', vals, grads, precision=hi).reshape(BR * K, BLK, D_IN)
        return (total.at[cols.reshape(-1)].add(terms), None)
    start = jnp.zeros((nbr, BLK, D_IN), jnp.float32)
    total, _ = lax.scan(backward_group, start, (col_groups, val_groups, dagg))
    return (hidden, weight_grad, bias_grad, total.reshape(NODES, D_IN))
```

```python
import math

import jax
import jax.numpy as jnp
from jax import lax
from jax.experimental import pallas as pl
from jax.experimental.pallas import tpu as pltpu
from jax.sharding import Mesh, PartitionSpec as P

BLK = 64
LANES = 128
VMEM_LIMIT = 40 * 1024 * 1024
PLANE = ("y", "x", "core")
WIDE = ("y", "z")
ALL = ("y", "z", "x", "core")
C0 = math.sqrt(2.0 / math.pi)
C1 = 0.044715


def split(value):
    high = value.astype(jnp.bfloat16)
    low = (value - high.astype(jnp.float32)).astype(jnp.bfloat16)
    return high, low


def dot(lhs, rhs, dims=((1,), (0,))):
    return lax.dot_general(lhs, rhs, (dims, ((), ())), preferred_element_type=jnp.float32)


def vmem(count):
    return [pl.BlockSpec(memory_space=pltpu.VMEM)] * count


def params():
    return pltpu.CompilerParams(vmem_limit_bytes=VMEM_LIMIT)


def prepare_kernel(counts, blocks, weight, stacked, turned, weight_rows, weight_low, weight_turned):
    rows, _, width = blocks.shape
    slot = lax.broadcasted_iota(jnp.int32, (BLK, width), 1) // BLK
    for r in range(rows):
        masked = jnp.where(slot < counts[r], blocks[r], 0.0)
        high, low = split(masked)
        stacked[r, :BLK, :] = high
        stacked[r, BLK:, :] = low
        both = jnp.concatenate([masked, masked - high.astype(jnp.float32)], axis=0)
        turned[r] = both.T.astype(jnp.bfloat16)
    high, low = split(weight[...])
    depth = weight.shape[0]
    weight_rows[:depth, :] = high
    weight_rows[depth:, :] = high
    weight_low[...] = low
    turned_high, turned_low = split(weight[...].T)
    weight_turned[:, :depth] = turned_high
    weight_turned[:, depth:] = turned_low


def prepare(counts, blocks, weight):
    rows, _, width = blocks.shape
    depth, hid = weight.shape
    half = jnp.bfloat16
    return pl.pallas_call(
        prepare_kernel,
        out_shape=(
            jax.ShapeDtypeStruct((rows, 2 * BLK, width), half),
            jax.ShapeDtypeStruct((rows, width, 2 * BLK), half),
            jax.ShapeDtypeStruct((2 * depth, hid), half),
            jax.ShapeDtypeStruct((depth, hid), half),
            jax.ShapeDtypeStruct((hid, 2 * depth), half),
        ),
        in_specs=[pl.BlockSpec(memory_space=pltpu.SMEM)] + vmem(2),
        out_specs=vmem(5),
        compiler_params=params(),
        cost_estimate=pl.CostEstimate(flops=2_000_000, bytes_accessed=4_000_000, transcendentals=0),
        name="prepare",
    )(counts, blocks, weight)


def layer_kernel(
    places, stacked, p0, p1, p2, p3, p4, p5, weight_rows, weight_low, weight_turned, bias, cotangent,
    hidden, sums, grads, band, picked, aggregated, sems,
):
    pieces = (p0, p1, p2, p3, p4, p5)
    span = p0.shape[0]
    copies = [
        pltpu.make_async_copy(piece, band.at[pl.ds(i * span, span)], sems.at[i])
        for i, piece in enumerate(pieces)
    ]
    for copy in copies:
        copy.start()
    for copy in copies:
        copy.wait()
    rows, _, width = stacked.shape
    slots = width // BLK
    depth = aggregated.shape[1]
    for r in range(rows):
        for k in range(slots):
            start = pl.multiple_of(places[r * slots + k] * BLK, BLK)
            high, low = split(band[pl.ds(start, BLK), :])
            picked[r % 2, k * BLK:(k + 1) * BLK, :depth] = high
            picked[r % 2, k * BLK:(k + 1) * BLK, depth:] = low
        product = dot(stacked[r], picked[r % 2])
        product = product[:BLK] + product[BLK:]
        aggregated[r * BLK:(r + 1) * BLK, :] = product[:, :depth] + product[:, depth:]
    value = aggregated[...]
    high, low = split(value)
    preact = dot(jnp.concatenate([high, low], axis=1), weight_rows[...]) + dot(high, weight_low[...])
    preact = preact + bias[...]
    square = preact * preact
    slope = jnp.tanh(C0 * (preact + C1 * (square * preact)))
    hidden[...] = 0.5 * preact * (1.0 + slope)
    local = 0.5 * (1.0 + slope) + 0.5 * preact * (1.0 - slope * slope) * (C0 * (1.0 + 3.0 * C1 * square))
    dpre = cotangent[...] * local
    dhigh, dlow = split(dpre)
    hid = dpre.shape[1]
    over_rows = ((0,), (0,))
    outer = dot(jnp.concatenate([value, value - high.astype(jnp.float32)], axis=1).T.astype(jnp.bfloat16), dhigh)
    outer = outer[:depth] + outer[depth:] + dot(value.T.astype(jnp.bfloat16), dlow)
    total = jnp.sum(dpre, axis=0, keepdims=True)
    shards = sums.shape[0]
    per = LANES * 2 // shards
    sums[:, :, per * LANES:] = jnp.zeros((shards, 1, LANES), jnp.float32)
    for d in range(shards):
        for j in range(per):
            row = d * per + j
            side, at = row // depth, row % depth
            sums[d, :, j * LANES:(j + 1) * LANES] = outer[at:at + 1, side * LANES:(side + 1) * LANES]
    for side in range(2):
        sums[side, :, per * LANES:] = total[:, side * LANES:(side + 1) * LANES]
    back = dot(jnp.concatenate([dhigh, dlow], axis=0), weight_turned[...])
    count = dpre.shape[0]
    back = back[:count] + back[count:]
    back = back[:, :depth] + back[:, depth:]
    bhigh, blow = split(back)
    for r in range(rows):
        for top in (0, BLK):
            grads[r, top:top + BLK, :depth] = bhigh[r * BLK:(r + 1) * BLK]
            grads[r, top:top + BLK, depth:] = blow[r * BLK:(r + 1) * BLK]


def layer(places, stacked, pieces, weight_rows, weight_low, weight_turned, bias, cotangent, shards):
    rows, _, width = stacked.shape
    span, depth = pieces[0].shape
    count, hid = cotangent.shape
    return pl.pallas_call(
        layer_kernel,
        out_shape=(
            jax.ShapeDtypeStruct((count, hid), jnp.float32),
            jax.ShapeDtypeStruct((shards, 1, depth * hid // shards + LANES), jnp.float32),
            jax.ShapeDtypeStruct((rows, 2 * BLK, 2 * depth), jnp.bfloat16),
        ),
        in_specs=[pl.BlockSpec(memory_space=pltpu.SMEM)] + vmem(1)
        + [pl.BlockSpec(memory_space=pl.ANY)] * 6 + vmem(5),
        out_specs=vmem(3),
        scratch_shapes=[
            pltpu.VMEM((6 * span, depth), jnp.float32),
            pltpu.VMEM((2, width, 2 * depth), jnp.bfloat16),
            pltpu.VMEM((count, depth), jnp.float32),
            pltpu.SemaphoreType.DMA((6,)),
        ],
        compiler_params=params(),
        cost_estimate=pl.CostEstimate(flops=400_000_000, bytes_accessed=6_000_000, transcendentals=65536),
        name="layer",
    )(places, stacked, *pieces, weight_rows, weight_low, weight_turned, bias, cotangent)


def spread_kernel(places, turned, grads, other, before, own, after, band, sems):
    rows, width, _ = turned.shape
    slots = width // BLK
    depth = band.shape[1]
    span = before.shape[0]
    band[...] = jnp.zeros_like(band)
    for r in range(rows):
        product = dot(turned[r], grads[r])
        product = product[:, :depth] + product[:, depth:]
        for k in range(slots):
            start = pl.multiple_of(places[r * slots + k] * BLK, BLK)
            where = pl.ds(start, BLK)
            band[where, :] = band[where, :] + product[k * BLK:(k + 1) * BLK]
    copies = [pltpu.make_async_copy(band.at[pl.ds(0, 3 * span)], other, sems.at[0])] + [
        pltpu.make_async_copy(band.at[pl.ds((3 + i) * span, span)], piece, sems.at[1 + i])
        for i, piece in enumerate((before, own, after))
    ]
    for copy in copies:
        copy.start()
    for copy in copies:
        copy.wait()


def spread(places, turned, grads, span, depth):
    piece = jax.ShapeDtypeStruct((span, depth), jnp.float32)
    return pl.pallas_call(
        spread_kernel,
        out_shape=(jax.ShapeDtypeStruct((3 * span, depth), jnp.float32), piece, piece, piece),
        in_specs=[pl.BlockSpec(memory_space=pltpu.SMEM)] + vmem(2),
        out_specs=[pl.BlockSpec(memory_space=pl.ANY)] * 4,
        scratch_shapes=[
            pltpu.VMEM((6 * span, depth), jnp.float32),
            pltpu.SemaphoreType.DMA((4,)),
        ],
        compiler_params=params(),
        cost_estimate=pl.CostEstimate(flops=300_000_000, bytes_accessed=5_000_000, transcendentals=0),
        name="spread",
    )(places, turned, grads)


def sum_kernel(parts, out):
    out[...] = jnp.broadcast_to(jnp.sum(parts[...], axis=0, keepdims=True), out.shape)


def sum_for_all(parts, shards):
    return pl.pallas_call(
        sum_kernel,
        out_shape=jax.ShapeDtypeStruct((shards,) + parts.shape[1:], parts.dtype),
        in_specs=vmem(1),
        out_specs=pl.BlockSpec(memory_space=pltpu.VMEM),
        compiler_params=params(),
        name="sum_for_all",
    )(parts)


def unpack_kernel(parts, outer, total):
    shards = parts.shape[0]
    depth = outer.shape[0]
    per = LANES * 2 // shards
    for d in range(shards):
        for j in range(per):
            row = d * per + j
            side, at = row // depth, row % depth
            outer[at:at + 1, side * LANES:(side + 1) * LANES] = parts[d, :, j * LANES:(j + 1) * LANES]
    for side in range(2):
        total[:, side * LANES:(side + 1) * LANES] = parts[side, :, per * LANES:]


def unpack(parts, depth, hid):
    return pl.pallas_call(
        unpack_kernel,
        out_shape=(
            jax.ShapeDtypeStruct((depth, hid), jnp.float32),
            jax.ShapeDtypeStruct((1, hid), jnp.float32),
        ),
        in_specs=vmem(1),
        out_specs=vmem(2),
        compiler_params=params(),
        name="unpack",
    )(parts)


def swap_cores(value):
    return lax.ppermute(value, "core", [(0, 1), (1, 0)])


def along_wide(value, step):
    count = lax.axis_size(WIDE)
    route = [(i, i + step) for i in range(count) if 0 <= i + step < count]
    return lax.ppermute(value, WIDE, route)


def body(features, columns, counts, blocks, weight, bias, cotangent):
    rows, depth = features.shape
    hid = weight.shape[1]
    chips = lax.axis_size("x")
    cores = lax.axis_size("core")
    shards = lax.axis_size(PLANE)
    levels = lax.axis_size("z")
    block_rows = columns.shape[0]
    stripe = block_rows * chips * cores
    span = chips * rows

    local = columns - (lax.axis_index(WIDE) - 1) * stripe
    part = local // stripe
    within = local % stripe
    device = within // block_rows
    foreign = (device % cores) ^ lax.axis_index("core")
    piece = (1 - foreign) * 3 + part
    places = (piece * (chips * block_rows) + (device // cores) * block_rows + within % block_rows).reshape(-1)

    row_of_chips = jnp.broadcast_to(features[None], (chips, rows, depth))
    own = lax.all_to_all(row_of_chips, "x", 0, 0).reshape(span, depth)
    before = along_wide(own, 1)
    after = along_wide(own, -1)
    own_other = swap_cores(own)
    before_other = swap_cores(before)
    after_other = swap_cores(after)
    stacked, turned, weight_rows, weight_low, weight_turned = prepare(counts, blocks, weight)
    pieces = (before_other, own_other, after_other, before, own, after)
    hidden, sums, grads = layer(
        places, stacked, pieces, weight_rows, weight_low, weight_turned, bias[None], cotangent, shards
    )

    other, to_before, to_own, to_after = spread(places, turned, grads, span, depth)
    from_core = swap_cores(other)
    from_after = along_wide(to_before + from_core[:span], -1)
    from_before = along_wide(to_after + from_core[2 * span:], 1)
    total = to_own + from_core[span:2 * span] + from_after + from_before
    shares = lax.all_to_all(total.reshape(chips, rows, depth), "x", 0, 0)
    feature_grad = jnp.sum(shares, axis=0)

    scattered = lax.all_to_all(sums, PLANE, 0, 0)
    scattered = lax.all_to_all(sum_for_all(scattered, levels), "z", 0, 0)
    gathered = lax.all_to_all(sum_for_all(scattered, shards), PLANE, 0, 0)
    weight_grad, bias_grad = unpack(gathered, depth, hid)
    return (hidden, weight_grad, bias_grad.reshape(hid), feature_grad)


def solution(mesh):
    wide, narrow = mesh.devices.shape
    levels = 32 if wide % 32 == 0 else wide // 2
    fine = Mesh(mesh.devices.reshape(wide // levels, levels, narrow // 2, 2), ALL)
    nodes = P(ALL, None)
    return jax.shard_map(
        body,
        mesh=fine,
        in_specs=(nodes, nodes, P(ALL), P(ALL, None, None), P(), P(), nodes),
        out_specs=(nodes, P(), P(), nodes),
        check_vma=False,
    )
```

```python
import math

import jax
import jax.numpy as jnp
from jax import lax
from jax.experimental import pallas as pl
from jax.experimental.pallas import tpu as pltpu
from jax.sharding import Mesh, PartitionSpec as P

BLK = 64
LANES = 128
VMEM_LIMIT = 40 * 1024 * 1024
WIDE = ("y", "far", "near")
ALL = ("y", "far", "near", "x", "core")
GROUP = ("y", "near", "x", "core")
C0 = math.sqrt(2.0 / math.pi)
C1 = 0.044715


def split(value):
    high = value.astype(jnp.bfloat16)
    low = (value - high.astype(jnp.float32)).astype(jnp.bfloat16)
    return high, low


def dot(lhs, rhs, dims=((1,), (0,))):
    return lax.dot_general(lhs, rhs, (dims, ((), ())), preferred_element_type=jnp.float32)


def vmem(count):
    return [pl.BlockSpec(memory_space=pltpu.VMEM)] * count


def params():
    return pltpu.CompilerParams(vmem_limit_bytes=VMEM_LIMIT)


def prepare_kernel(counts, blocks, weight, stacked, turned, weight_rows, weight_low, weight_turned):
    rows, _, width = blocks.shape
    slot = lax.broadcasted_iota(jnp.int32, (BLK, width), 1) // BLK
    for r in range(rows):
        masked = jnp.where(slot < counts[r], blocks[r], 0.0)
        high, low = split(masked)
        stacked[r, :BLK, :] = high
        stacked[r, BLK:, :] = low
        both = jnp.concatenate([masked, masked - high.astype(jnp.float32)], axis=0)
        turned[r] = both.T.astype(jnp.bfloat16)
    high, low = split(weight[...])
    depth = weight.shape[0]
    weight_rows[:depth, :] = high
    weight_rows[depth:, :] = high
    weight_low[...] = low
    turned_high, turned_low = split(weight[...].T)
    weight_turned[:, :depth] = turned_high
    weight_turned[:, depth:] = turned_low


def prepare(counts, blocks, weight):
    rows, _, width = blocks.shape
    depth, hid = weight.shape
    half = jnp.bfloat16
    return pl.pallas_call(
        prepare_kernel,
        out_shape=(
            jax.ShapeDtypeStruct((rows, 2 * BLK, width), half),
            jax.ShapeDtypeStruct((rows, width, 2 * BLK), half),
            jax.ShapeDtypeStruct((2 * depth, hid), half),
            jax.ShapeDtypeStruct((depth, hid), half),
            jax.ShapeDtypeStruct((hid, 2 * depth), half),
        ),
        in_specs=[pl.BlockSpec(memory_space=pltpu.SMEM)] + vmem(2),
        out_specs=vmem(5),
        compiler_params=params(),
        cost_estimate=pl.CostEstimate(flops=2_000_000, bytes_accessed=4_000_000, transcendentals=0),
        name="prepare",
    )(counts, blocks, weight)


def layer_kernel(
    places, stacked, p0, p1, p2, p3, p4, p5, weight_rows, weight_low, weight_turned, bias, cotangent,
    hidden, sums, grads, band, picked, aggregated, sems,
):
    pieces = (p0, p1, p2, p3, p4, p5)
    span = p0.shape[0]
    copies = [
        pltpu.make_async_copy(piece, band.at[pl.ds(i * span, span)], sems.at[i])
        for i, piece in enumerate(pieces)
    ]
    for copy in copies:
        copy.start()
    for copy in copies:
        copy.wait()
    rows, _, width = stacked.shape
    slots = width // BLK
    depth = aggregated.shape[1]
    for r in range(rows):
        for k in range(slots):
            start = pl.multiple_of(places[r * slots + k] * BLK, BLK)
            high, low = split(band[pl.ds(start, BLK), :])
            picked[r % 2, k * BLK:(k + 1) * BLK, :depth] = high
            picked[r % 2, k * BLK:(k + 1) * BLK, depth:] = low
        product = dot(stacked[r], picked[r % 2])
        product = product[:BLK] + product[BLK:]
        aggregated[r * BLK:(r + 1) * BLK, :] = product[:, :depth] + product[:, depth:]
    value = aggregated[...]
    high, low = split(value)
    preact = dot(jnp.concatenate([high, low], axis=1), weight_rows[...]) + dot(high, weight_low[...])
    preact = preact + bias[...]
    square = preact * preact
    slope = jnp.tanh(C0 * (preact + C1 * (square * preact)))
    hidden[...] = 0.5 * preact * (1.0 + slope)
    local = 0.5 * (1.0 + slope) + 0.5 * preact * (1.0 - slope * slope) * (C0 * (1.0 + 3.0 * C1 * square))
    dpre = cotangent[...] * local
    dhigh, dlow = split(dpre)
    hid = dpre.shape[1]
    over_rows = ((0,), (0,))
    outer = dot(jnp.concatenate([value, value - high.astype(jnp.float32)], axis=1).T.astype(jnp.bfloat16), dhigh)
    outer = outer[:depth] + outer[depth:] + dot(value.T.astype(jnp.bfloat16), dlow)
    total = jnp.sum(dpre, axis=0, keepdims=True)
    shards = sums.shape[0]
    per = LANES * 2 // shards
    sums[:, :, per * LANES:] = jnp.zeros((shards, 1, LANES), jnp.float32)
    for d in range(shards):
        for j in range(per):
            row = d * per + j
            side, at = row // depth, row % depth
            sums[d, :, j * LANES:(j + 1) * LANES] = outer[at:at + 1, side * LANES:(side + 1) * LANES]
    for side in range(2):
        sums[side, :, per * LANES:] = total[:, side * LANES:(side + 1) * LANES]
    back = dot(jnp.concatenate([dhigh, dlow], axis=0), weight_turned[...])
    count = dpre.shape[0]
    back = back[:count] + back[count:]
    back = back[:, :depth] + back[:, depth:]
    bhigh, blow = split(back)
    for r in range(rows):
        for top in (0, BLK):
            grads[r, top:top + BLK, :depth] = bhigh[r * BLK:(r + 1) * BLK]
            grads[r, top:top + BLK, depth:] = blow[r * BLK:(r + 1) * BLK]


def layer(places, stacked, pieces, weight_rows, weight_low, weight_turned, bias, cotangent, shards):
    rows, _, width = stacked.shape
    span, depth = pieces[0].shape
    count, hid = cotangent.shape
    return pl.pallas_call(
        layer_kernel,
        out_shape=(
            jax.ShapeDtypeStruct((count, hid), jnp.float32),
            jax.ShapeDtypeStruct((shards, 1, depth * hid // shards + LANES), jnp.float32),
            jax.ShapeDtypeStruct((rows, 2 * BLK, 2 * depth), jnp.bfloat16),
        ),
        in_specs=[pl.BlockSpec(memory_space=pltpu.SMEM)] + vmem(1)
        + [pl.BlockSpec(memory_space=pl.ANY)] * 6 + vmem(5),
        out_specs=vmem(3),
        scratch_shapes=[
            pltpu.VMEM((6 * span, depth), jnp.float32),
            pltpu.VMEM((2, width, 2 * depth), jnp.bfloat16),
            pltpu.VMEM((count, depth), jnp.float32),
            pltpu.SemaphoreType.DMA((6,)),
        ],
        compiler_params=params(),
        cost_estimate=pl.CostEstimate(flops=400_000_000, bytes_accessed=6_000_000, transcendentals=65536),
        name="layer",
    )(places, stacked, *pieces, weight_rows, weight_low, weight_turned, bias, cotangent)


def spread_kernel(targets, turned, grads, other, mine, band, sems):
    rows, width, _ = turned.shape
    slots = width // BLK
    half, depth = mine.shape
    band[...] = jnp.zeros_like(band)
    for r in range(rows):
        product = dot(turned[r], grads[r])
        product = product[:, :depth] + product[:, depth:]
        for k in range(slots):
            start = pl.multiple_of(targets[r * slots + k] * BLK, BLK)
            where = pl.ds(start, BLK)
            band[where, :] = band[where, :] + product[k * BLK:(k + 1) * BLK]
    copies = [
        pltpu.make_async_copy(band.at[pl.ds(i * half, half)], piece, sems.at[i])
        for i, piece in enumerate((other, mine))
    ]
    for copy in copies:
        copy.start()
    for copy in copies:
        copy.wait()


def spread(targets, turned, grads, half, depth):
    piece = jax.ShapeDtypeStruct((half, depth), jnp.float32)
    return pl.pallas_call(
        spread_kernel,
        out_shape=(piece, piece),
        in_specs=[pl.BlockSpec(memory_space=pltpu.SMEM)] + vmem(2),
        out_specs=[pl.BlockSpec(memory_space=pl.ANY)] * 2,
        scratch_shapes=[
            pltpu.VMEM((2 * half, depth), jnp.float32),
            pltpu.SemaphoreType.DMA((2,)),
        ],
        compiler_params=params(),
        cost_estimate=pl.CostEstimate(flops=300_000_000, bytes_accessed=5_000_000, transcendentals=0),
        name="spread",
    )(targets, turned, grads)


def sum_kernel(parts, out):
    out[...] = jnp.broadcast_to(jnp.sum(parts[...], axis=0, keepdims=True), out.shape)


def sum_for_all(parts, shards):
    return pl.pallas_call(
        sum_kernel,
        out_shape=jax.ShapeDtypeStruct((shards,) + parts.shape[1:], parts.dtype),
        in_specs=vmem(1),
        out_specs=pl.BlockSpec(memory_space=pltpu.VMEM),
        compiler_params=params(),
        name="sum_for_all",
    )(parts)


def unpack_kernel(parts, outer, total):
    shards = parts.shape[0]
    depth = outer.shape[0]
    per = LANES * 2 // shards
    for d in range(shards):
        for j in range(per):
            row = d * per + j
            side, at = row // depth, row % depth
            outer[at:at + 1, side * LANES:(side + 1) * LANES] = parts[d, :, j * LANES:(j + 1) * LANES]
    for side in range(2):
        total[:, side * LANES:(side + 1) * LANES] = parts[side, :, per * LANES:]


def unpack(parts, depth, hid):
    return pl.pallas_call(
        unpack_kernel,
        out_shape=(
            jax.ShapeDtypeStruct((depth, hid), jnp.float32),
            jax.ShapeDtypeStruct((1, hid), jnp.float32),
        ),
        in_specs=vmem(1),
        out_specs=vmem(2),
        compiler_params=params(),
        name="unpack",
    )(parts)


def swap_cores(value):
    return lax.ppermute(value, "core", [(0, 1), (1, 0)])


def along_wide(value, step):
    count = lax.axis_size(WIDE)
    route = [(i, i + step) for i in range(count) if 0 <= i + step < count]
    return lax.ppermute(value, WIDE, route)


def body(features, columns, counts, blocks, weight, bias, cotangent):
    rows, depth = features.shape
    hid = weight.shape[1]
    chips = lax.axis_size("x")
    cores = lax.axis_size("core")
    shards = lax.axis_size(GROUP)
    levels = lax.axis_size("far")
    block_rows = columns.shape[0]
    stripe = block_rows * chips * cores
    span = chips * rows

    local = columns - (lax.axis_index(WIDE) - 1) * stripe
    part = local // stripe
    within = local % stripe
    device = within // block_rows
    block = within % block_rows
    chip = device // cores
    mine = 1 - ((device % cores) ^ lax.axis_index("core"))
    places = (((mine * 3 + part) * chips + chip) * block_rows + block).reshape(-1)
    targets = (((mine * chips + chip) * 3 + part) * block_rows + block).reshape(-1)

    row_of_chips = jnp.broadcast_to(features[None], (chips, rows, depth))
    own = lax.all_to_all(row_of_chips, "x", 0, 0).reshape(span, depth)
    before = along_wide(own, 1)
    after = along_wide(own, -1)
    own_other = swap_cores(own)
    before_other = swap_cores(before)
    after_other = swap_cores(after)
    stacked, turned, weight_rows, weight_low, weight_turned = prepare(counts, blocks, weight)
    pieces = (before_other, own_other, after_other, before, own, after)
    hidden, sums, grads = layer(
        places, stacked, pieces, weight_rows, weight_low, weight_turned, bias[None], cotangent, shards
    )

    scattered = lax.all_to_all(sums, GROUP, 0, 0)
    scattered = lax.all_to_all(sum_for_all(scattered, levels), "far", 0, 0)
    gathered = lax.all_to_all(sum_for_all(scattered, shards), GROUP, 0, 0)
    weight_grad, bias_grad = unpack(gathered, depth, hid)

    to_other, to_mine = spread(targets, turned, grads, 3 * span, depth)
    total = to_mine + swap_cores(to_other)
    share = lax.psum_scatter(total, "x", scatter_dimension=0, tiled=True)
    from_after = along_wide(share[:rows], -1)
    from_before = along_wide(share[2 * rows:], 1)
    feature_grad = share[rows:2 * rows] + from_after + from_before
    return (hidden, weight_grad, bias_grad.reshape(hid), feature_grad)


def solution(mesh):
    wide, narrow = mesh.devices.shape
    levels = 32 if wide % 32 == 0 else wide // 2
    fine = Mesh(mesh.devices.reshape(wide // levels, levels // 2, 2, narrow // 2, 2), ALL)
    nodes = P(ALL, None)
    return jax.shard_map(
        body,
        mesh=fine,
        in_specs=(nodes, nodes, P(ALL), P(ALL, None, None), P(), P(), nodes),
        out_specs=(nodes, P(), P(), nodes),
        check_vma=False,
    )
```

```python
import math

import jax
import jax.numpy as jnp
from jax import lax
from jax.experimental import pallas as pl
from jax.experimental.pallas import tpu as pltpu
from jax.sharding import Mesh, PartitionSpec as P

BLK = 64
LANES = 128
VMEM_LIMIT = 40 * 1024 * 1024
WIDE = ("y", "far", "near")
ALL = ("y", "far", "near", "x", "core")
GROUP = ("y", "near", "x", "core")
C0 = math.sqrt(2.0 / math.pi)
C1 = 0.044715


def split(value):
    high = value.astype(jnp.bfloat16)
    low = (value - high.astype(jnp.float32)).astype(jnp.bfloat16)
    return high, low


def dot(lhs, rhs, dims=((1,), (0,))):
    return lax.dot_general(lhs, rhs, (dims, ((), ())), preferred_element_type=jnp.float32)


def vmem(count):
    return [pl.BlockSpec(memory_space=pltpu.VMEM)] * count


def params():
    return pltpu.CompilerParams(vmem_limit_bytes=VMEM_LIMIT)


def prepare_kernel(counts, blocks, weight, stacked, turned, weight_rows, weight_low, weight_turned):
    rows, _, width = blocks.shape
    slot = lax.broadcasted_iota(jnp.int32, (BLK, width), 1) // BLK
    for r in range(rows):
        masked = jnp.where(slot < counts[r], blocks[r], 0.0)
        high, low = split(masked)
        stacked[r, :BLK, :] = high
        stacked[r, BLK:, :] = low
        both = jnp.concatenate([masked, masked - high.astype(jnp.float32)], axis=0)
        turned[r] = both.T.astype(jnp.bfloat16)
    high, low = split(weight[...])
    depth = weight.shape[0]
    weight_rows[:depth, :] = high
    weight_rows[depth:, :] = high
    weight_low[...] = low
    turned_high, turned_low = split(weight[...].T)
    weight_turned[:, :depth] = turned_high
    weight_turned[:, depth:] = turned_low


def prepare(counts, blocks, weight):
    rows, _, width = blocks.shape
    depth, hid = weight.shape
    half = jnp.bfloat16
    return pl.pallas_call(
        prepare_kernel,
        out_shape=(
            jax.ShapeDtypeStruct((rows, 2 * BLK, width), half),
            jax.ShapeDtypeStruct((rows, width, 2 * BLK), half),
            jax.ShapeDtypeStruct((2 * depth, hid), half),
            jax.ShapeDtypeStruct((depth, hid), half),
            jax.ShapeDtypeStruct((hid, 2 * depth), half),
        ),
        in_specs=[pl.BlockSpec(memory_space=pltpu.SMEM)] + vmem(2),
        out_specs=vmem(5),
        compiler_params=params(),
        cost_estimate=pl.CostEstimate(flops=2_000_000, bytes_accessed=4_000_000, transcendentals=0),
        name="prepare",
    )(counts, blocks, weight)


def layer_kernel(
    places, stacked, p0, p1, p2, p3, p4, p5, weight_rows, weight_low, weight_turned, bias, cotangent,
    hidden, sums, grads, band, picked, aggregated, sems,
):
    pieces = (p0, p1, p2, p3, p4, p5)
    span = p0.shape[0]
    copies = [
        pltpu.make_async_copy(piece, band.at[pl.ds(i * span, span)], sems.at[i])
        for i, piece in enumerate(pieces)
    ]
    for copy in copies:
        copy.start()
    for copy in copies:
        copy.wait()
    rows, _, width = stacked.shape
    slots = width // BLK
    depth = aggregated.shape[1]
    for r in range(rows):
        for k in range(slots):
            start = pl.multiple_of(places[r * slots + k] * BLK, BLK)
            high, low = split(band[pl.ds(start, BLK), :])
            picked[r % 2, k * BLK:(k + 1) * BLK, :depth] = high
            picked[r % 2, k * BLK:(k + 1) * BLK, depth:] = low
        product = dot(stacked[r], picked[r % 2])
        product = product[:BLK] + product[BLK:]
        aggregated[r * BLK:(r + 1) * BLK, :] = product[:, :depth] + product[:, depth:]
    value = aggregated[...]
    high, low = split(value)
    preact = dot(jnp.concatenate([high, low], axis=1), weight_rows[...]) + dot(high, weight_low[...])
    preact = preact + bias[...]
    square = preact * preact
    slope = jnp.tanh(C0 * (preact + C1 * (square * preact)))
    hidden[...] = 0.5 * preact * (1.0 + slope)
    local = 0.5 * (1.0 + slope) + 0.5 * preact * (1.0 - slope * slope) * (C0 * (1.0 + 3.0 * C1 * square))
    dpre = cotangent[...] * local
    dhigh, dlow = split(dpre)
    hid = dpre.shape[1]
    over_rows = ((0,), (0,))
    outer = dot(jnp.concatenate([value, value - high.astype(jnp.float32)], axis=1).T.astype(jnp.bfloat16), dhigh)
    outer = outer[:depth] + outer[depth:] + dot(value.T.astype(jnp.bfloat16), dlow)
    total = jnp.sum(dpre, axis=0, keepdims=True)
    shards = sums.shape[0]
    per = LANES * 2 // shards
    sums[:, :, per * LANES:] = jnp.zeros((shards, 1, LANES), jnp.float32)
    for d in range(shards):
        for j in range(per):
            row = d * per + j
            side, at = row // depth, row % depth
            sums[d, :, j * LANES:(j + 1) * LANES] = outer[at:at + 1, side * LANES:(side + 1) * LANES]
    for side in range(2):
        sums[side, :, per * LANES:] = total[:, side * LANES:(side + 1) * LANES]
    back = dot(jnp.concatenate([dhigh, dlow], axis=0), weight_turned[...])
    count = dpre.shape[0]
    back = back[:count] + back[count:]
    back = back[:, :depth] + back[:, depth:]
    bhigh, blow = split(back)
    for r in range(rows):
        for top in (0, BLK):
            grads[r, top:top + BLK, :depth] = bhigh[r * BLK:(r + 1) * BLK]
            grads[r, top:top + BLK, depth:] = blow[r * BLK:(r + 1) * BLK]


def layer(places, stacked, pieces, weight_rows, weight_low, weight_turned, bias, cotangent, shards):
    rows, _, width = stacked.shape
    span, depth = pieces[0].shape
    count, hid = cotangent.shape
    return pl.pallas_call(
        layer_kernel,
        out_shape=(
            jax.ShapeDtypeStruct((count, hid), jnp.float32),
            jax.ShapeDtypeStruct((shards, 1, depth * hid // shards + LANES), jnp.float32),
            jax.ShapeDtypeStruct((rows, 2 * BLK, 2 * depth), jnp.bfloat16),
        ),
        in_specs=[pl.BlockSpec(memory_space=pltpu.SMEM)] + vmem(1)
        + [pl.BlockSpec(memory_space=pl.ANY)] * 6 + vmem(5),
        out_specs=vmem(3),
        scratch_shapes=[
            pltpu.VMEM((6 * span, depth), jnp.float32),
            pltpu.VMEM((2, width, 2 * depth), jnp.bfloat16),
            pltpu.VMEM((count, depth), jnp.float32),
            pltpu.SemaphoreType.DMA((6,)),
        ],
        compiler_params=params(),
        cost_estimate=pl.CostEstimate(flops=400_000_000, bytes_accessed=6_000_000, transcendentals=65536),
        name="layer",
    )(places, stacked, *pieces, weight_rows, weight_low, weight_turned, bias, cotangent)


def spread_kernel(targets, turned, grads, other, mine, band, sems):
    rows, width, _ = turned.shape
    slots = width // BLK
    half, depth = mine.shape
    band[...] = jnp.zeros_like(band)
    for r in range(rows):
        product = dot(turned[r], grads[r])
        product = product[:, :depth] + product[:, depth:]
        for k in range(slots):
            start = pl.multiple_of(targets[r * slots + k] * BLK, BLK)
            where = pl.ds(start, BLK)
            band[where, :] = band[where, :] + product[k * BLK:(k + 1) * BLK]
    copies = [
        pltpu.make_async_copy(band.at[pl.ds(i * half, half)], piece, sems.at[i])
        for i, piece in enumerate((other, mine))
    ]
    for copy in copies:
        copy.start()
    for copy in copies:
        copy.wait()


def spread(targets, turned, grads, half, depth):
    piece = jax.ShapeDtypeStruct((half, depth), jnp.float32)
    return pl.pallas_call(
        spread_kernel,
        out_shape=(piece, piece),
        in_specs=[pl.BlockSpec(memory_space=pltpu.SMEM)] + vmem(2),
        out_specs=[pl.BlockSpec(memory_space=pl.ANY)] * 2,
        scratch_shapes=[
            pltpu.VMEM((2 * half, depth), jnp.float32),
            pltpu.SemaphoreType.DMA((2,)),
        ],
        compiler_params=params(),
        cost_estimate=pl.CostEstimate(flops=300_000_000, bytes_accessed=5_000_000, transcendentals=0),
        name="spread",
    )(targets, turned, grads)


def sum_kernel(parts, *refs):
    out = refs[-1]
    out[...] = jnp.broadcast_to(jnp.sum(parts[...], axis=0, keepdims=True), out.shape)


def sum_for_all(parts, shards, *behind):
    return pl.pallas_call(
        sum_kernel,
        out_shape=jax.ShapeDtypeStruct((shards,) + parts.shape[1:], parts.dtype),
        in_specs=vmem(1) + [pl.BlockSpec(memory_space=pl.ANY)] * len(behind),
        out_specs=pl.BlockSpec(memory_space=pltpu.VMEM),
        compiler_params=params(),
        name="sum_for_all",
    )(parts, *behind)


def unpack_kernel(parts, outer, total):
    shards = parts.shape[0]
    depth = outer.shape[0]
    per = LANES * 2 // shards
    for d in range(shards):
        for j in range(per):
            row = d * per + j
            side, at = row // depth, row % depth
            outer[at:at + 1, side * LANES:(side + 1) * LANES] = parts[d, :, j * LANES:(j + 1) * LANES]
    for side in range(2):
        total[:, side * LANES:(side + 1) * LANES] = parts[side, :, per * LANES:]


def unpack(parts, depth, hid):
    return pl.pallas_call(
        unpack_kernel,
        out_shape=(
            jax.ShapeDtypeStruct((depth, hid), jnp.float32),
            jax.ShapeDtypeStruct((1, hid), jnp.float32),
        ),
        in_specs=vmem(1),
        out_specs=vmem(2),
        compiler_params=params(),
        name="unpack",
    )(parts)


def swap_cores(value):
    return lax.ppermute(value, "core", [(0, 1), (1, 0)])


def along_wide(value, step):
    count = lax.axis_size(WIDE)
    route = [(i, i + step) for i in range(count) if 0 <= i + step < count]
    return lax.ppermute(value, WIDE, route)


def body(features, columns, counts, blocks, weight, bias, cotangent):
    rows, depth = features.shape
    hid = weight.shape[1]
    chips = lax.axis_size("x")
    cores = lax.axis_size("core")
    shards = lax.axis_size(GROUP)
    levels = lax.axis_size("far")
    block_rows = columns.shape[0]
    stripe = block_rows * chips * cores
    span = chips * rows

    local = columns - (lax.axis_index(WIDE) - 1) * stripe
    part = local // stripe
    within = local % stripe
    device = within // block_rows
    block = within % block_rows
    chip = device // cores
    mine = 1 - ((device % cores) ^ lax.axis_index("core"))
    places = (((mine * 3 + part) * chips + chip) * block_rows + block).reshape(-1)
    ahead = lax.rem(chip - lax.axis_index("x") + chips, chips)
    targets = (((mine * 3 + part) * chips + ahead) * block_rows + block).reshape(-1)

    row_of_chips = jnp.broadcast_to(features[None], (chips, rows, depth))
    own = lax.all_to_all(row_of_chips, "x", 0, 0).reshape(span, depth)
    before = along_wide(own, 1)
    after = along_wide(own, -1)
    own_other = swap_cores(own)
    before_other = swap_cores(before)
    after_other = swap_cores(after)
    stacked, turned, weight_rows, weight_low, weight_turned = prepare(counts, blocks, weight)
    pieces = (before_other, own_other, after_other, before, own, after)
    hidden, sums, grads = layer(
        places, stacked, pieces, weight_rows, weight_low, weight_turned, bias[None], cotangent, shards
    )

    to_other, to_mine = spread(targets, turned, grads, 3 * span, depth)
    from_core = swap_cores(to_other)
    from_after = along_wide(to_mine[:span] + from_core[:span], -1)
    from_before = along_wide(to_mine[2 * span:] + from_core[2 * span:], 1)
    shares = []
    for step in range(chips):
        chunk = slice(rows * step, rows * (step + 1))
        at = slice(span + rows * step, span + rows * (step + 1))
        share = to_mine[at] + from_core[at] + from_after[chunk] + from_before[chunk]
        if step:
            share = lax.ppermute(share, "x", [(i, (i + step) % chips) for i in range(chips)])
        shares.append(share)
    feature_grad = sum(shares[1:], shares[0])
    scattered = lax.all_to_all(sums, GROUP, 0, 0)
    scattered = lax.all_to_all(sum_for_all(scattered, levels), "far", 0, 0)
    gathered = lax.all_to_all(sum_for_all(scattered, shards, *shares[1::2]), GROUP, 0, 0)
    weight_grad, bias_grad = unpack(gathered, depth, hid)

    return (hidden, weight_grad, bias_grad.reshape(hid), feature_grad)


def solution(mesh):
    wide, narrow = mesh.devices.shape
    levels = 32 if wide % 32 == 0 else wide // 2
    fine = Mesh(mesh.devices.reshape(wide // levels, levels // 2, 2, narrow // 2, 2), ALL)
    nodes = P(ALL, None)
    return jax.shard_map(
        body,
        mesh=fine,
        in_specs=(nodes, nodes, P(ALL), P(ALL, None, None), P(), P(), nodes),
        out_specs=(nodes, P(), P(), nodes),
        check_vma=False,
    )
```

```python
import functools
import math

import jax
import jax.numpy as jnp
from jax import lax
from jax.experimental import pallas as pl
from jax.experimental.pallas import tpu as pltpu
from jax.sharding import Mesh, PartitionSpec as P

BLK = 64
LANES = 128
MIB = 1024 * 1024
WIDE = ("y", "far", "near")
ALL = ("y", "far", "near", "x", "core")
GROUP = ("y", "near", "x", "core")
C0 = math.sqrt(2.0 / math.pi)
C1 = 0.044715


def split(value):
    high = value.astype(jnp.bfloat16)
    low = (value - high.astype(jnp.float32)).astype(jnp.bfloat16)
    return high, low


def dot(lhs, rhs, dims=((1,), (0,))):
    return lax.dot_general(lhs, rhs, (dims, ((), ())), preferred_element_type=jnp.float32)


def vmem(count):
    return [pl.BlockSpec(memory_space=pltpu.VMEM)] * count


def params(mib):
    return pltpu.CompilerParams(vmem_limit_bytes=mib * MIB)


def prepare_kernel(
    chips, cores, counts, columns, blocks, weight,
    places, targets, stacked, turned, weight_rows, weight_low, weight_turned,
):
    rows, _, width = blocks.shape
    stripe = rows * chips * cores
    local = columns[...] - (lax.axis_index(WIDE) - 1) * stripe
    part = local >> (stripe.bit_length() - 1)
    block = local & (rows - 1)
    device = (local & (stripe - 1)) >> (rows.bit_length() - 1)
    chip = device >> (cores.bit_length() - 1)
    mine = ((device ^ lax.axis_index("core")) & (cores - 1)) ^ 1
    band = mine * 3 + part
    ahead = (chip - lax.axis_index("x")) & (chips - 1)
    places[...] = (band * chips + chip) * rows + block
    targets[...] = (band * chips + ahead) * rows + block
    slot = lax.broadcasted_iota(jnp.int32, (BLK, width), 1) // BLK
    for r in range(rows):
        masked = jnp.where(slot < counts[r], blocks[r], 0.0)
        high, low = split(masked)
        stacked[r, :BLK, :] = high
        stacked[r, BLK:, :] = low
        both = jnp.concatenate([masked, masked - high.astype(jnp.float32)], axis=0)
        turned[r] = both.T.astype(jnp.bfloat16)
    high, low = split(weight[...])
    depth = weight.shape[0]
    weight_rows[:depth, :] = high
    weight_rows[depth:, :] = high
    weight_low[...] = low
    turned_high, turned_low = split(weight[...].T)
    weight_turned[:, :depth] = turned_high
    weight_turned[:, depth:] = turned_low


def prepare(counts, columns, blocks, weight):
    rows, _, width = blocks.shape
    index = jax.ShapeDtypeStruct(columns.shape, columns.dtype)
    depth, hid = weight.shape
    half = jnp.bfloat16
    return pl.pallas_call(
        functools.partial(prepare_kernel, lax.axis_size("x"), lax.axis_size("core")),
        out_shape=(
            index,
            index,
            jax.ShapeDtypeStruct((rows, 2 * BLK, width), half),
            jax.ShapeDtypeStruct((rows, width, 2 * BLK), half),
            jax.ShapeDtypeStruct((2 * depth, hid), half),
            jax.ShapeDtypeStruct((depth, hid), half),
            jax.ShapeDtypeStruct((hid, 2 * depth), half),
        ),
        in_specs=[pl.BlockSpec(memory_space=pltpu.SMEM)] + vmem(3),
        out_specs=vmem(7),
        compiler_params=params(12),
        cost_estimate=pl.CostEstimate(flops=2_000_000, bytes_accessed=4_000_000, transcendentals=0),
        name="prepare",
    )(counts, columns, blocks, weight)


def layer_kernel(
    places, stacked, p0, p1, p2, p3, p4, p5, weight_rows, weight_low, weight_turned, bias, cotangent,
    hidden, sums, grads, band, picked, aggregated, sems,
):
    pieces = (p0, p1, p2, p3, p4, p5)
    span = p0.shape[0]
    copies = [
        pltpu.make_async_copy(piece, band.at[pl.ds(i * span, span)], sems.at[i])
        for i, piece in enumerate(pieces)
    ]
    for copy in copies:
        copy.start()
    for copy in copies:
        copy.wait()
    rows, _, width = stacked.shape
    slots = width // BLK
    depth = aggregated.shape[1]
    for r in range(rows):
        for k in range(slots):
            start = pl.multiple_of(places[r, k] * BLK, BLK)
            high, low = split(band[pl.ds(start, BLK), :])
            picked[r % 2, k * BLK:(k + 1) * BLK, :depth] = high
            picked[r % 2, k * BLK:(k + 1) * BLK, depth:] = low
        product = dot(stacked[r], picked[r % 2])
        product = product[:BLK] + product[BLK:]
        aggregated[r * BLK:(r + 1) * BLK, :] = product[:, :depth] + product[:, depth:]
    value = aggregated[...]
    high, low = split(value)
    preact = dot(jnp.concatenate([high, low], axis=1), weight_rows[...]) + dot(high, weight_low[...])
    preact = preact + bias[...]
    square = preact * preact
    slope = jnp.tanh(C0 * (preact + C1 * (square * preact)))
    hidden[...] = 0.5 * preact * (1.0 + slope)
    local = 0.5 * (1.0 + slope) + 0.5 * preact * (1.0 - slope * slope) * (C0 * (1.0 + 3.0 * C1 * square))
    dpre = cotangent[...] * local
    dhigh, dlow = split(dpre)
    hid = dpre.shape[1]
    over_rows = ((0,), (0,))
    outer = dot(jnp.concatenate([value, value - high.astype(jnp.float32)], axis=1).T.astype(jnp.bfloat16), dhigh)
    outer = outer[:depth] + outer[depth:] + dot(value.T.astype(jnp.bfloat16), dlow)
    total = jnp.sum(dpre, axis=0, keepdims=True)
    shards = sums.shape[0]
    per = LANES * 2 // shards
    sums[:, :, per * LANES:] = jnp.zeros((shards, 1, LANES), jnp.float32)
    for d in range(shards):
        for j in range(per):
            row = d * per + j
            side, at = row // depth, row % depth
            sums[d, :, j * LANES:(j + 1) * LANES] = outer[at:at + 1, side * LANES:(side + 1) * LANES]
    for side in range(2):
        sums[side, :, per * LANES:] = total[:, side * LANES:(side + 1) * LANES]
    back = dot(jnp.concatenate([dhigh, dlow], axis=0), weight_turned[...])
    count = dpre.shape[0]
    back = back[:count] + back[count:]
    back = back[:, :depth] + back[:, depth:]
    bhigh, blow = split(back)
    for r in range(rows):
        for top in (0, BLK):
            grads[r, top:top + BLK, :depth] = bhigh[r * BLK:(r + 1) * BLK]
            grads[r, top:top + BLK, depth:] = blow[r * BLK:(r + 1) * BLK]


def layer(places, stacked, pieces, weight_rows, weight_low, weight_turned, bias, cotangent, shards):
    rows, _, width = stacked.shape
    span, depth = pieces[0].shape
    count, hid = cotangent.shape
    return pl.pallas_call(
        layer_kernel,
        out_shape=(
            jax.ShapeDtypeStruct((count, hid), jnp.float32),
            jax.ShapeDtypeStruct((shards, 1, depth * hid // shards + LANES), jnp.float32),
            jax.ShapeDtypeStruct((rows, 2 * BLK, 2 * depth), jnp.bfloat16),
        ),
        in_specs=[pl.BlockSpec(memory_space=pltpu.SMEM)] + vmem(1)
        + [pl.BlockSpec(memory_space=pl.ANY)] * 6 + vmem(5),
        out_specs=vmem(3),
        scratch_shapes=[
            pltpu.VMEM((6 * span, depth), jnp.float32),
            pltpu.VMEM((2, width, 2 * depth), jnp.bfloat16),
            pltpu.VMEM((count, depth), jnp.float32),
            pltpu.SemaphoreType.DMA((6,)),
        ],
        compiler_params=params(16),
        cost_estimate=pl.CostEstimate(flops=400_000_000, bytes_accessed=6_000_000, transcendentals=65536),
        name="layer",
    )(places, stacked, *pieces, weight_rows, weight_low, weight_turned, bias, cotangent)


def spread_kernel(targets, turned, grads, other, mine, band, sems):
    rows, width, _ = turned.shape
    slots = width // BLK
    half, depth = mine.shape
    band[...] = jnp.zeros_like(band)
    for r in range(rows):
        product = dot(turned[r], grads[r])
        product = product[:, :depth] + product[:, depth:]
        for k in range(slots):
            start = pl.multiple_of(targets[r, k] * BLK, BLK)
            where = pl.ds(start, BLK)
            band[where, :] = band[where, :] + product[k * BLK:(k + 1) * BLK]
    copies = [
        pltpu.make_async_copy(band.at[pl.ds(i * half, half)], piece, sems.at[i])
        for i, piece in enumerate((other, mine))
    ]
    for copy in copies:
        copy.start()
    for copy in copies:
        copy.wait()


def spread(targets, turned, grads, half, depth):
    piece = jax.ShapeDtypeStruct((half, depth), jnp.float32)
    return pl.pallas_call(
        spread_kernel,
        out_shape=(piece, piece),
        in_specs=[pl.BlockSpec(memory_space=pltpu.SMEM)] + vmem(2),
        out_specs=[pl.BlockSpec(memory_space=pl.ANY)] * 2,
        scratch_shapes=[
            pltpu.VMEM((2 * half, depth), jnp.float32),
            pltpu.SemaphoreType.DMA((2,)),
        ],
        compiler_params=params(12),
        cost_estimate=pl.CostEstimate(flops=300_000_000, bytes_accessed=5_000_000, transcendentals=0),
        name="spread",
    )(targets, turned, grads)


def sum_kernel(parts, *refs):
    out = refs[-1]
    out[...] = jnp.broadcast_to(jnp.sum(parts[...], axis=0, keepdims=True), out.shape)


def sum_for_all(parts, shards, *behind):
    return pl.pallas_call(
        sum_kernel,
        out_shape=jax.ShapeDtypeStruct((shards,) + parts.shape[1:], parts.dtype),
        in_specs=vmem(1) + [pl.BlockSpec(memory_space=pl.ANY)] * len(behind),
        out_specs=pl.BlockSpec(memory_space=pltpu.VMEM),
        compiler_params=params(4),
        name="sum_for_all",
    )(parts, *behind)


def unpack_kernel(parts, outer, total):
    shards = parts.shape[0]
    depth = outer.shape[0]
    per = LANES * 2 // shards
    for d in range(shards):
        for j in range(per):
            row = d * per + j
            side, at = row // depth, row % depth
            outer[at:at + 1, side * LANES:(side + 1) * LANES] = parts[d, :, j * LANES:(j + 1) * LANES]
    for side in range(2):
        total[:, side * LANES:(side + 1) * LANES] = parts[side, :, per * LANES:]


def unpack(parts, depth, hid):
    return pl.pallas_call(
        unpack_kernel,
        out_shape=(
            jax.ShapeDtypeStruct((depth, hid), jnp.float32),
            jax.ShapeDtypeStruct((1, hid), jnp.float32),
        ),
        in_specs=vmem(1),
        out_specs=vmem(2),
        compiler_params=params(4),
        name="unpack",
    )(parts)


def swap_cores(value):
    return lax.ppermute(value, "core", [(0, 1), (1, 0)])


def along_wide(value, step):
    count = lax.axis_size(WIDE)
    route = [(i, i + step) for i in range(count) if 0 <= i + step < count]
    return lax.ppermute(value, WIDE, route)


def body(features, columns, counts, blocks, weight, bias, cotangent):
    rows, depth = features.shape
    hid = weight.shape[1]
    chips = lax.axis_size("x")
    shards = lax.axis_size(GROUP)
    levels = lax.axis_size("far")
    span = chips * rows

    row_of_chips = jnp.broadcast_to(features[None], (chips, rows, depth))
    own = lax.all_to_all(row_of_chips, "x", 0, 0).reshape(span, depth)
    before = along_wide(own, 1)
    after = along_wide(own, -1)
    own_other = swap_cores(own)
    before_other = swap_cores(before)
    after_other = swap_cores(after)
    places, targets, stacked, turned, weight_rows, weight_low, weight_turned = prepare(
        counts, columns, blocks, weight
    )
    pieces = (before_other, own_other, after_other, before, own, after)
    hidden, sums, grads = layer(
        places, stacked, pieces, weight_rows, weight_low, weight_turned, bias[None], cotangent, shards
    )

    to_other, to_mine = spread(targets, turned, grads, 3 * span, depth)
    from_core = swap_cores(to_other)
    from_after = along_wide(to_mine[:span] + from_core[:span], -1)
    from_before = along_wide(to_mine[2 * span:] + from_core[2 * span:], 1)
    shares = []
    for step in range(chips):
        chunk = slice(rows * step, rows * (step + 1))
        at = slice(span + rows * step, span + rows * (step + 1))
        share = to_mine[at] + from_core[at] + from_after[chunk] + from_before[chunk]
        if step:
            share = lax.ppermute(share, "x", [(i, (i + step) % chips) for i in range(chips)])
        shares.append(share)
    feature_grad = sum(shares[1:], shares[0])
    scattered = lax.all_to_all(sums, GROUP, 0, 0)
    scattered = lax.all_to_all(sum_for_all(scattered, levels), "far", 0, 0)
    gathered = lax.all_to_all(sum_for_all(scattered, shards, *shares[1:]), GROUP, 0, 0)
    weight_grad, bias_grad = unpack(gathered, depth, hid)

    return (hidden, weight_grad, bias_grad.reshape(hid), feature_grad)


def solution(mesh):
    wide, narrow = mesh.devices.shape
    levels = 32 if wide % 32 == 0 else wide // 2
    fine = Mesh(mesh.devices.reshape(wide // levels, levels // 2, 2, narrow // 2, 2), ALL)
    nodes = P(ALL, None)
    return jax.shard_map(
        body,
        mesh=fine,
        in_specs=(nodes, nodes, P(ALL), P(ALL, None, None), P(), P(), nodes),
        out_specs=(nodes, P(), P(), nodes),
        check_vma=False,
    )
```

```python
import functools
import math

import jax
import jax.numpy as jnp
from jax import lax
from jax.experimental import pallas as pl
from jax.experimental.pallas import tpu as pltpu
from jax.sharding import Mesh, PartitionSpec as P

BLK = 64
LANES = 128
MIB = 1024 * 1024
WIDE = ("y", "far", "near")
ALL = ("y", "far", "near", "x", "core")
GROUP = ("y", "near", "x", "core")
C0 = math.sqrt(2.0 / math.pi)
C1 = 0.044715


def split(value):
    high = value.astype(jnp.bfloat16)
    low = (value - high.astype(jnp.float32)).astype(jnp.bfloat16)
    return high, low


def dot(lhs, rhs, dims=((1,), (0,))):
    return lax.dot_general(lhs, rhs, (dims, ((), ())), preferred_element_type=jnp.float32)


def vmem(count):
    return [pl.BlockSpec(memory_space=pltpu.VMEM)] * count


def params(mib):
    return pltpu.CompilerParams(vmem_limit_bytes=mib * MIB)


def prepare_kernel(
    chips, cores, counts, columns, blocks, weight,
    places, targets, stacked, turned, weight_rows, weight_low, weight_turned,
):
    rows, _, width = blocks.shape
    stripe = rows * chips * cores
    local = columns[...] - (lax.axis_index(WIDE) - 1) * stripe
    part = local >> (stripe.bit_length() - 1)
    block = local & (rows - 1)
    device = (local & (stripe - 1)) >> (rows.bit_length() - 1)
    chip = device >> (cores.bit_length() - 1)
    mine = ((device ^ lax.axis_index("core")) & (cores - 1)) ^ 1
    band = mine * 3 + part
    ahead = (chip - lax.axis_index("x")) & (chips - 1)
    places[...] = (band * chips + chip) * rows + block
    targets[...] = ((mine * chips + ahead) * 3 + part) * rows + block
    slot = lax.broadcasted_iota(jnp.int32, (BLK, width), 1) // BLK
    for r in range(rows):
        masked = jnp.where(slot < counts[r], blocks[r], 0.0)
        high, low = split(masked)
        stacked[r, :BLK, :] = high
        stacked[r, BLK:, :] = low
        both = jnp.concatenate([masked, masked - high.astype(jnp.float32)], axis=0)
        turned[r] = both.T.astype(jnp.bfloat16)
    high, low = split(weight[...])
    depth = weight.shape[0]
    weight_rows[:depth, :] = high
    weight_rows[depth:, :] = high
    weight_low[...] = low
    turned_high, turned_low = split(weight[...].T)
    weight_turned[:, :depth] = turned_high
    weight_turned[:, depth:] = turned_low


def prepare(counts, columns, blocks, weight):
    rows, _, width = blocks.shape
    index = jax.ShapeDtypeStruct(columns.shape, columns.dtype)
    depth, hid = weight.shape
    half = jnp.bfloat16
    return pl.pallas_call(
        functools.partial(prepare_kernel, lax.axis_size("x"), lax.axis_size("core")),
        out_shape=(
            index,
            index,
            jax.ShapeDtypeStruct((rows, 2 * BLK, width), half),
            jax.ShapeDtypeStruct((rows, width, 2 * BLK), half),
            jax.ShapeDtypeStruct((2 * depth, hid), half),
            jax.ShapeDtypeStruct((depth, hid), half),
            jax.ShapeDtypeStruct((hid, 2 * depth), half),
        ),
        in_specs=[pl.BlockSpec(memory_space=pltpu.SMEM)] + vmem(3),
        out_specs=vmem(7),
        compiler_params=params(12),
        cost_estimate=pl.CostEstimate(flops=2_000_000, bytes_accessed=4_000_000, transcendentals=0),
        name="prepare",
    )(counts, columns, blocks, weight)


def layer_kernel(
    places, stacked, p0, p1, p2, p3, p4, p5, weight_rows, weight_low, weight_turned, bias, cotangent,
    hidden, sums, grads, band, picked, aggregated, sems,
):
    pieces = (p0, p1, p2, p3, p4, p5)
    span = p0.shape[0]
    copies = [
        pltpu.make_async_copy(piece, band.at[pl.ds(i * span, span)], sems.at[i])
        for i, piece in enumerate(pieces)
    ]
    for copy in copies:
        copy.start()
    for copy in copies:
        copy.wait()
    rows, _, width = stacked.shape
    slots = width // BLK
    depth = aggregated.shape[1]
    for r in range(rows):
        for k in range(slots):
            start = pl.multiple_of(places[r, k] * BLK, BLK)
            high, low = split(band[pl.ds(start, BLK), :])
            picked[r % 2, k * BLK:(k + 1) * BLK, :depth] = high
            picked[r % 2, k * BLK:(k + 1) * BLK, depth:] = low
        product = dot(stacked[r], picked[r % 2])
        product = product[:BLK] + product[BLK:]
        aggregated[r * BLK:(r + 1) * BLK, :] = product[:, :depth] + product[:, depth:]
    value = aggregated[...]
    high, low = split(value)
    preact = dot(jnp.concatenate([high, low], axis=1), weight_rows[...]) + dot(high, weight_low[...])
    preact = preact + bias[...]
    square = preact * preact
    slope = jnp.tanh(C0 * (preact + C1 * (square * preact)))
    hidden[...] = 0.5 * preact * (1.0 + slope)
    local = 0.5 * (1.0 + slope) + 0.5 * preact * (1.0 - slope * slope) * (C0 * (1.0 + 3.0 * C1 * square))
    dpre = cotangent[...] * local
    dhigh, dlow = split(dpre)
    hid = dpre.shape[1]
    over_rows = ((0,), (0,))
    outer = dot(jnp.concatenate([value, value - high.astype(jnp.float32)], axis=1).T.astype(jnp.bfloat16), dhigh)
    outer = outer[:depth] + outer[depth:] + dot(value.T.astype(jnp.bfloat16), dlow)
    total = jnp.sum(dpre, axis=0, keepdims=True)
    shards = sums.shape[0]
    per = LANES * 2 // shards
    sums[:, :, per * LANES:] = jnp.zeros((shards, 1, LANES), jnp.float32)
    for d in range(shards):
        for j in range(per):
            row = d * per + j
            side, at = row // depth, row % depth
            sums[d, :, j * LANES:(j + 1) * LANES] = outer[at:at + 1, side * LANES:(side + 1) * LANES]
    for side in range(2):
        sums[side, :, per * LANES:] = total[:, side * LANES:(side + 1) * LANES]
    back = dot(jnp.concatenate([dhigh, dlow], axis=0), weight_turned[...])
    count = dpre.shape[0]
    back = back[:count] + back[count:]
    back = back[:, :depth] + back[:, depth:]
    bhigh, blow = split(back)
    for r in range(rows):
        for top in (0, BLK):
            grads[r, top:top + BLK, :depth] = bhigh[r * BLK:(r + 1) * BLK]
            grads[r, top:top + BLK, depth:] = blow[r * BLK:(r + 1) * BLK]


def layer(places, stacked, pieces, weight_rows, weight_low, weight_turned, bias, cotangent, shards):
    rows, _, width = stacked.shape
    span, depth = pieces[0].shape
    count, hid = cotangent.shape
    return pl.pallas_call(
        layer_kernel,
        out_shape=(
            jax.ShapeDtypeStruct((count, hid), jnp.float32),
            jax.ShapeDtypeStruct((shards, 1, depth * hid // shards + LANES), jnp.float32),
            jax.ShapeDtypeStruct((rows, 2 * BLK, 2 * depth), jnp.bfloat16),
        ),
        in_specs=[pl.BlockSpec(memory_space=pltpu.SMEM)] + vmem(1)
        + [pl.BlockSpec(memory_space=pl.ANY)] * 6 + vmem(5),
        out_specs=vmem(3),
        scratch_shapes=[
            pltpu.VMEM((6 * span, depth), jnp.float32),
            pltpu.VMEM((2, width, 2 * depth), jnp.bfloat16),
            pltpu.VMEM((count, depth), jnp.float32),
            pltpu.SemaphoreType.DMA((6,)),
        ],
        compiler_params=params(16),
        cost_estimate=pl.CostEstimate(flops=400_000_000, bytes_accessed=6_000_000, transcendentals=65536),
        name="layer",
    )(places, stacked, *pieces, weight_rows, weight_low, weight_turned, bias, cotangent)


def spread_kernel(targets, turned, grads, other, mine, band, sems):
    rows, width, _ = turned.shape
    slots = width // BLK
    half, depth = mine.shape
    band[...] = jnp.zeros_like(band)
    for r in range(rows):
        product = dot(turned[r], grads[r])
        product = product[:, :depth] + product[:, depth:]
        for k in range(slots):
            start = pl.multiple_of(targets[r, k] * BLK, BLK)
            where = pl.ds(start, BLK)
            band[where, :] = band[where, :] + product[k * BLK:(k + 1) * BLK]
    copies = [
        pltpu.make_async_copy(band.at[pl.ds(i * half, half)], piece, sems.at[i])
        for i, piece in enumerate((other, mine))
    ]
    for copy in copies:
        copy.start()
    for copy in copies:
        copy.wait()


def spread(targets, turned, grads, half, depth):
    piece = jax.ShapeDtypeStruct((half, depth), jnp.float32)
    return pl.pallas_call(
        spread_kernel,
        out_shape=(piece, piece),
        in_specs=[pl.BlockSpec(memory_space=pltpu.SMEM)] + vmem(2),
        out_specs=[pl.BlockSpec(memory_space=pl.ANY)] * 2,
        scratch_shapes=[
            pltpu.VMEM((2 * half, depth), jnp.float32),
            pltpu.SemaphoreType.DMA((2,)),
        ],
        compiler_params=params(12),
        cost_estimate=pl.CostEstimate(flops=300_000_000, bytes_accessed=5_000_000, transcendentals=0),
        name="spread",
    )(targets, turned, grads)


def sum_kernel(parts, *refs):
    out = refs[-1]
    out[...] = jnp.broadcast_to(jnp.sum(parts[...], axis=0, keepdims=True), out.shape)


def sum_for_all(parts, shards, *behind):
    return pl.pallas_call(
        sum_kernel,
        out_shape=jax.ShapeDtypeStruct((shards,) + parts.shape[1:], parts.dtype),
        in_specs=vmem(1) + [pl.BlockSpec(memory_space=pl.ANY)] * len(behind),
        out_specs=pl.BlockSpec(memory_space=pltpu.VMEM),
        compiler_params=params(4),
        name="sum_for_all",
    )(parts, *behind)


def unpack_kernel(parts, outer, total):
    shards = parts.shape[0]
    depth = outer.shape[0]
    per = LANES * 2 // shards
    for d in range(shards):
        for j in range(per):
            row = d * per + j
            side, at = row // depth, row % depth
            outer[at:at + 1, side * LANES:(side + 1) * LANES] = parts[d, :, j * LANES:(j + 1) * LANES]
    for side in range(2):
        total[:, side * LANES:(side + 1) * LANES] = parts[side, :, per * LANES:]


def unpack(parts, depth, hid):
    return pl.pallas_call(
        unpack_kernel,
        out_shape=(
            jax.ShapeDtypeStruct((depth, hid), jnp.float32),
            jax.ShapeDtypeStruct((1, hid), jnp.float32),
        ),
        in_specs=vmem(1),
        out_specs=vmem(2),
        compiler_params=params(4),
        name="unpack",
    )(parts)


def swap_cores(value):
    return lax.ppermute(value, "core", [(0, 1), (1, 0)])


def along_wide(value, step):
    count = lax.axis_size(WIDE)
    route = [(i, i + step) for i in range(count) if 0 <= i + step < count]
    return lax.ppermute(value, WIDE, route)


def body(features, columns, counts, blocks, weight, bias, cotangent):
    rows, depth = features.shape
    hid = weight.shape[1]
    chips = lax.axis_size("x")
    shards = lax.axis_size(GROUP)
    levels = lax.axis_size("far")
    span = chips * rows

    row_of_chips = jnp.broadcast_to(features[None], (chips, rows, depth))
    own = lax.all_to_all(row_of_chips, "x", 0, 0).reshape(span, depth)
    before = along_wide(own, 1)
    after = along_wide(own, -1)
    own_other = swap_cores(own)
    before_other = swap_cores(before)
    after_other = swap_cores(after)
    places, targets, stacked, turned, weight_rows, weight_low, weight_turned = prepare(
        counts, columns, blocks, weight
    )
    pieces = (before_other, own_other, after_other, before, own, after)
    hidden, sums, grads = layer(
        places, stacked, pieces, weight_rows, weight_low, weight_turned, bias[None], cotangent, shards
    )

    to_other, to_mine = spread(targets, turned, grads, 3 * span, depth)
    from_core = swap_cores(to_other)
    size = 3 * rows
    half = size // 2

    def chunk(step, low, high):
        at = slice(step * size + low, step * size + high)
        return to_mine[at] + from_core[at]

    forth = [(i, (i + 1) % chips) for i in range(chips)]
    back = [(i, (i - 1) % chips) for i in range(chips)]
    by_next = lax.ppermute(chunk(2, 0, half), "x", forth)
    by_last = lax.ppermute(chunk(2, half, size), "x", back)

    scattered = lax.all_to_all(sums, GROUP, 0, 0)
    plane_sum = sum_for_all(scattered, levels, by_next, by_last)
    scattered = lax.all_to_all(plane_sum, "far", 0, 0)

    low_last = lax.ppermute(chunk(1, 0, half) + by_next, "x", forth)
    high_last = lax.ppermute(chunk(1, half, size), "x", forth)
    low_next = lax.ppermute(chunk(3, 0, half), "x", back)
    high_next = lax.ppermute(chunk(3, half, size) + by_last, "x", back)
    before = chunk(0, 0, rows) + low_last[:rows] + low_next[:rows]
    rest = half - rows
    own_low = chunk(0, rows, half) + low_last[rows:] + low_next[rows:]
    own_high = chunk(0, half, 2 * rows) + high_last[:rows - rest] + high_next[:rows - rest]
    after = chunk(0, 2 * rows, size) + high_last[rows - rest:] + high_next[rows - rest:]
    from_after = along_wide(before, -1)
    from_before = along_wide(after, 1)
    feature_grad = jnp.concatenate([own_low, own_high]) + from_after + from_before

    gathered = lax.all_to_all(sum_for_all(scattered, shards, low_last, high_last, low_next, high_next), GROUP, 0, 0)
    weight_grad, bias_grad = unpack(gathered, depth, hid)

    return (hidden, weight_grad, bias_grad.reshape(hid), feature_grad)


def solution(mesh):
    wide, narrow = mesh.devices.shape
    levels = 32 if wide % 32 == 0 else wide // 2
    fine = Mesh(mesh.devices.reshape(wide // levels, levels // 2, 2, narrow // 2, 2), ALL)
    nodes = P(ALL, None)
    return jax.shard_map(
        body,
        mesh=fine,
        in_specs=(nodes, nodes, P(ALL), P(ALL, None, None), P(), P(), nodes),
        out_specs=(nodes, P(), P(), nodes),
        check_vma=False,
    )
```

```python
import functools
import math

import jax
import jax.numpy as jnp
from jax import lax
from jax.experimental import pallas as pl
from jax.experimental.pallas import tpu as pltpu
from jax.sharding import Mesh, PartitionSpec as P

BLK = 64
LANES = 128
MIB = 1024 * 1024
WIDE = ("y", "far", "near")
ALL = ("y", "far", "near", "x", "core")
GROUP = ("y", "near", "x", "core")
C0 = math.sqrt(2.0 / math.pi)
C1 = 0.044715


def split(value):
    high = value.astype(jnp.bfloat16)
    low = (value - high.astype(jnp.float32)).astype(jnp.bfloat16)
    return high, low


def dot(lhs, rhs, dims=((1,), (0,))):
    return lax.dot_general(lhs, rhs, (dims, ((), ())), preferred_element_type=jnp.float32)


def vmem(count):
    return [pl.BlockSpec(memory_space=pltpu.VMEM)] * count


def params(mib):
    return pltpu.CompilerParams(vmem_limit_bytes=mib * MIB)


def prepare_kernel(
    chips, cores, counts, columns, blocks, weight,
    places, targets, stacked, turned, weight_rows, weight_low, weight_turned,
):
    rows, _, width = blocks.shape
    stripe = rows * chips * cores
    local = columns[...] - (lax.axis_index(WIDE) - 1) * stripe
    part = local >> (stripe.bit_length() - 1)
    block = local & (rows - 1)
    device = (local & (stripe - 1)) >> (rows.bit_length() - 1)
    chip = device >> (cores.bit_length() - 1)
    mine = ((device ^ lax.axis_index("core")) & (cores - 1)) ^ 1
    band = mine * 3 + part
    ahead = (chip - lax.axis_index("x")) & (chips - 1)
    places[...] = (band * chips + chip) * rows + block
    targets[...] = (band * chips + ahead) * rows + block
    slot = lax.broadcasted_iota(jnp.int32, (BLK, width), 1) // BLK
    for r in range(rows):
        masked = jnp.where(slot < counts[r], blocks[r], 0.0)
        high, low = split(masked)
        stacked[r, :BLK, :] = high
        stacked[r, BLK:, :] = low
        both = jnp.concatenate([masked, masked - high.astype(jnp.float32)], axis=0)
        turned[r] = both.T.astype(jnp.bfloat16)
    high, low = split(weight[...])
    depth = weight.shape[0]
    weight_rows[:depth, :] = high
    weight_rows[depth:, :] = high
    weight_low[...] = low
    turned_high, turned_low = split(weight[...].T)
    weight_turned[:, :depth] = turned_high
    weight_turned[:, depth:] = turned_low


def prepare(counts, columns, blocks, weight):
    rows, _, width = blocks.shape
    index = jax.ShapeDtypeStruct(columns.shape, columns.dtype)
    depth, hid = weight.shape
    half = jnp.bfloat16
    return pl.pallas_call(
        functools.partial(prepare_kernel, lax.axis_size("x"), lax.axis_size("core")),
        out_shape=(
            index,
            index,
            jax.ShapeDtypeStruct((rows, 2 * BLK, width), half),
            jax.ShapeDtypeStruct((rows, width, 2 * BLK), half),
            jax.ShapeDtypeStruct((2 * depth, hid), half),
            jax.ShapeDtypeStruct((depth, hid), half),
            jax.ShapeDtypeStruct((hid, 2 * depth), half),
        ),
        in_specs=[pl.BlockSpec(memory_space=pltpu.SMEM)] + vmem(3),
        out_specs=vmem(7),
        compiler_params=params(12),
        cost_estimate=pl.CostEstimate(flops=2_000_000, bytes_accessed=4_000_000, transcendentals=0),
        name="prepare",
    )(counts, columns, blocks, weight)


def layer_kernel(
    places, targets, stacked, turned, p0, p1, p2, p3, p4, p5,
    weight_rows, weight_low, weight_turned, bias, cotangent,
    hidden, sums, other, mine, band, spread, picked, aggregated, grads, sems, out_sems,
):
    pieces = (p0, p1, p2, p3, p4, p5)
    span = p0.shape[0]
    copies = [
        pltpu.make_async_copy(piece, band.at[pl.ds(i * span, span)], sems.at[i])
        for i, piece in enumerate(pieces)
    ]
    for copy in copies:
        copy.start()
    spread[...] = jnp.zeros_like(spread)
    for copy in copies:
        copy.wait()
    rows, _, width = stacked.shape
    slots = width // BLK
    depth = aggregated.shape[1]
    for r in range(rows):
        for k in range(slots):
            start = pl.multiple_of(places[r, k] * BLK, BLK)
            high, low = split(band[pl.ds(start, BLK), :])
            picked[r % 2, k * BLK:(k + 1) * BLK, :depth] = high
            picked[r % 2, k * BLK:(k + 1) * BLK, depth:] = low
        product = dot(stacked[r], picked[r % 2])
        product = product[:BLK] + product[BLK:]
        aggregated[r * BLK:(r + 1) * BLK, :] = product[:, :depth] + product[:, depth:]
    value = aggregated[...]
    high, low = split(value)
    preact = dot(jnp.concatenate([high, low], axis=1), weight_rows[...]) + dot(high, weight_low[...])
    preact = preact + bias[...]
    square = preact * preact
    slope = jnp.tanh(C0 * (preact + C1 * (square * preact)))
    hidden[...] = 0.5 * preact * (1.0 + slope)
    local = 0.5 * (1.0 + slope) + 0.5 * preact * (1.0 - slope * slope) * (C0 * (1.0 + 3.0 * C1 * square))
    dpre = cotangent[...] * local
    dhigh, dlow = split(dpre)
    hid = dpre.shape[1]
    over_rows = ((0,), (0,))
    outer = dot(jnp.concatenate([value, value - high.astype(jnp.float32)], axis=1).T.astype(jnp.bfloat16), dhigh)
    outer = outer[:depth] + outer[depth:] + dot(value.T.astype(jnp.bfloat16), dlow)
    total = jnp.sum(dpre, axis=0, keepdims=True)
    shards = sums.shape[0]
    per = LANES * 2 // shards
    sums[:, :, per * LANES:] = jnp.zeros((shards, 1, LANES), jnp.float32)
    for d in range(shards):
        for j in range(per):
            row = d * per + j
            side, at = row // depth, row % depth
            sums[d, :, j * LANES:(j + 1) * LANES] = outer[at:at + 1, side * LANES:(side + 1) * LANES]
    for side in range(2):
        sums[side, :, per * LANES:] = total[:, side * LANES:(side + 1) * LANES]
    back = dot(jnp.concatenate([dhigh, dlow], axis=0), weight_turned[...])
    count = dpre.shape[0]
    back = back[:count] + back[count:]
    back = back[:, :depth] + back[:, depth:]
    bhigh, blow = split(back)
    for r in range(rows):
        for top in (0, BLK):
            grads[r, top:top + BLK, :depth] = bhigh[r * BLK:(r + 1) * BLK]
            grads[r, top:top + BLK, depth:] = blow[r * BLK:(r + 1) * BLK]
        product = dot(turned[r], grads[r])
        product = product[:, :depth] + product[:, depth:]
        for k in range(slots):
            where = pl.ds(pl.multiple_of(targets[r, k] * BLK, BLK), BLK)
            spread[where, :] = spread[where, :] + product[k * BLK:(k + 1) * BLK]
    half = other.shape[0]
    copies = [
        pltpu.make_async_copy(spread.at[pl.ds(i * half, half)], piece, out_sems.at[i])
        for i, piece in enumerate((other, mine))
    ]
    for copy in copies:
        copy.start()
    for copy in copies:
        copy.wait()


def layer(places, targets, stacked, turned, pieces, weight_rows, weight_low, weight_turned, bias, cotangent, shards):
    rows, _, width = stacked.shape
    span, depth = pieces[0].shape
    count, hid = cotangent.shape
    return pl.pallas_call(
        layer_kernel,
        out_shape=(
            jax.ShapeDtypeStruct((count, hid), jnp.float32),
            jax.ShapeDtypeStruct((shards, 1, depth * hid // shards + LANES), jnp.float32),
            jax.ShapeDtypeStruct((3 * span, depth), jnp.float32),
            jax.ShapeDtypeStruct((3 * span, depth), jnp.float32),
        ),
        in_specs=[pl.BlockSpec(memory_space=pltpu.SMEM)] * 2 + vmem(2)
        + [pl.BlockSpec(memory_space=pl.ANY)] * 6 + vmem(5),
        out_specs=vmem(2) + [pl.BlockSpec(memory_space=pl.ANY)] * 2,
        scratch_shapes=[
            pltpu.VMEM((6 * span, depth), jnp.float32),
            pltpu.VMEM((6 * span, depth), jnp.float32),
            pltpu.VMEM((2, width, 2 * depth), jnp.bfloat16),
            pltpu.VMEM((count, depth), jnp.float32),
            pltpu.VMEM((rows, 2 * BLK, 2 * depth), jnp.bfloat16),
            pltpu.SemaphoreType.DMA((6,)),
            pltpu.SemaphoreType.DMA((2,)),
        ],
        compiler_params=params(20),
        cost_estimate=pl.CostEstimate(flops=700_000_000, bytes_accessed=11_000_000, transcendentals=65536),
        name="layer",
    )(places, targets, stacked, turned, *pieces, weight_rows, weight_low, weight_turned, bias, cotangent)


def add_kernel(terms, from_core, before, own, after):
    span = own.shape[0]
    for part, out in enumerate((before, own, after)):
        at = slice(part * span, (part + 1) * span)
        out[...] = terms[at] + from_core[at]


def add_parts(terms, from_core):
    size, depth = terms.shape
    piece = jax.ShapeDtypeStruct((size // 3, depth), terms.dtype)
    return pl.pallas_call(
        add_kernel,
        out_shape=(piece, piece, piece),
        in_specs=vmem(2),
        out_specs=vmem(3),
        compiler_params=params(8),
        cost_estimate=pl.CostEstimate(flops=400_000, bytes_accessed=4_700_000, transcendentals=0),
        name="add_parts",
    )(terms, from_core)


def sum_kernel(parts, *refs):
    out = refs[-1]
    out[...] = jnp.broadcast_to(jnp.sum(parts[...], axis=0, keepdims=True), out.shape)


def sum_for_all(parts, shards, *behind):
    return pl.pallas_call(
        sum_kernel,
        out_shape=jax.ShapeDtypeStruct((shards,) + parts.shape[1:], parts.dtype),
        in_specs=vmem(1) + [pl.BlockSpec(memory_space=pl.ANY)] * len(behind),
        out_specs=pl.BlockSpec(memory_space=pltpu.VMEM),
        compiler_params=params(4),
        name="sum_for_all",
    )(parts, *behind)


def unpack_kernel(parts, outer, total):
    shards = parts.shape[0]
    depth = outer.shape[0]
    per = LANES * 2 // shards
    for d in range(shards):
        for j in range(per):
            row = d * per + j
            side, at = row // depth, row % depth
            outer[at:at + 1, side * LANES:(side + 1) * LANES] = parts[d, :, j * LANES:(j + 1) * LANES]
    for side in range(2):
        total[:, side * LANES:(side + 1) * LANES] = parts[side, :, per * LANES:]


def unpack(parts, depth, hid):
    return pl.pallas_call(
        unpack_kernel,
        out_shape=(
            jax.ShapeDtypeStruct((depth, hid), jnp.float32),
            jax.ShapeDtypeStruct((1, hid), jnp.float32),
        ),
        in_specs=vmem(1),
        out_specs=vmem(2),
        compiler_params=params(4),
        name="unpack",
    )(parts)


def swap_cores(value):
    return lax.ppermute(value, "core", [(0, 1), (1, 0)])


def along_wide(value, step):
    count = lax.axis_size(WIDE)
    route = [(i, i + step) for i in range(count) if 0 <= i + step < count]
    return lax.ppermute(value, WIDE, route)


def body(features, columns, counts, blocks, weight, bias, cotangent):
    rows, depth = features.shape
    hid = weight.shape[1]
    chips = lax.axis_size("x")
    shards = lax.axis_size(GROUP)
    levels = lax.axis_size("far")
    span = chips * rows

    row_of_chips = jnp.broadcast_to(features[None], (chips, rows, depth))
    own = lax.all_to_all(row_of_chips, "x", 0, 0).reshape(span, depth)
    before = along_wide(own, 1)
    after = along_wide(own, -1)
    own_other = swap_cores(own)
    before_other = swap_cores(before)
    after_other = swap_cores(after)
    places, targets, stacked, turned, weight_rows, weight_low, weight_turned = prepare(
        counts, columns, blocks, weight
    )
    pieces = (before_other, own_other, after_other, before, own, after)
    hidden, sums, to_other, to_mine = layer(
        places, targets, stacked, turned, pieces, weight_rows, weight_low, weight_turned, bias[None], cotangent, shards
    )

    to_before, to_own, to_after = add_parts(to_mine, swap_cores(to_other))
    from_after = along_wide(to_before, -1)
    from_before = along_wide(to_after, 1)
    shares = []
    for step in range(chips):
        chunk = slice(rows * step, rows * (step + 1))
        share = to_own[chunk] + from_after[chunk] + from_before[chunk]
        if step:
            share = lax.ppermute(share, "x", [(i, (i + step) % chips) for i in range(chips)])
        shares.append(share)
    feature_grad = sum(shares[1:], shares[0])
    scattered = lax.all_to_all(sums, GROUP, 0, 0)
    scattered = lax.all_to_all(sum_for_all(scattered, levels), "far", 0, 0)
    gathered = lax.all_to_all(sum_for_all(scattered, shards, *shares[1:]), GROUP, 0, 0)
    weight_grad, bias_grad = unpack(gathered, depth, hid)

    return (hidden, weight_grad, bias_grad.reshape(hid), feature_grad)


def solution(mesh):
    wide, narrow = mesh.devices.shape
    levels = 32 if wide % 32 == 0 else wide // 2
    fine = Mesh(mesh.devices.reshape(wide // levels, levels // 2, 2, narrow // 2, 2), ALL)
    nodes = P(ALL, None)
    return jax.shard_map(
        body,
        mesh=fine,
        in_specs=(nodes, nodes, P(ALL), P(ALL, None, None), P(), P(), nodes),
        out_specs=(nodes, P(), P(), nodes),
        check_vma=False,
    )
```

```python
import functools
import math

import jax
import jax.numpy as jnp
from jax import lax
from jax.experimental import pallas as pl
from jax.experimental.pallas import tpu as pltpu
from jax.sharding import Mesh, PartitionSpec as P

BLK = 64
LANES = 128
MIB = 1024 * 1024
WIDE = ("y", "far", "near")
ALL = ("y", "far", "near", "x", "core")
GROUP = ("y", "near", "x", "core")
C0 = math.sqrt(2.0 / math.pi)
C1 = 0.044715


def split(value):
    high = value.astype(jnp.bfloat16)
    low = (value - high.astype(jnp.float32)).astype(jnp.bfloat16)
    return high, low


def dot(lhs, rhs, dims=((1,), (0,))):
    return lax.dot_general(lhs, rhs, (dims, ((), ())), preferred_element_type=jnp.float32)


def vmem(count):
    return [pl.BlockSpec(memory_space=pltpu.VMEM)] * count


def params(mib):
    return pltpu.CompilerParams(vmem_limit_bytes=mib * MIB)


def prepare_kernel(
    chips, cores, counts, columns, blocks, weight,
    places, targets, stacked, turned, weight_rows, weight_low, weight_turned,
):
    rows, _, width = blocks.shape
    stripe = rows * chips * cores
    local = columns[...] - (lax.axis_index(WIDE) - 1) * stripe
    part = local >> (stripe.bit_length() - 1)
    block = local & (rows - 1)
    device = (local & (stripe - 1)) >> (rows.bit_length() - 1)
    chip = device >> (cores.bit_length() - 1)
    mine = ((device ^ lax.axis_index("core")) & (cores - 1)) ^ 1
    band = mine * 3 + part
    ahead = (chip - lax.axis_index("x")) & (chips - 1)
    places[...] = (band * chips + chip) * rows + block
    targets[...] = (band * chips + ahead) * rows + block
    slot = lax.broadcasted_iota(jnp.int32, (BLK, width), 1) // BLK
    for r in range(rows):
        masked = jnp.where(slot < counts[r], blocks[r], 0.0)
        high, low = split(masked)
        stacked[r, :BLK, :] = high
        stacked[r, BLK:, :] = low
        both = jnp.concatenate([masked, masked - high.astype(jnp.float32)], axis=0)
        turned[r] = both.T.astype(jnp.bfloat16)
    high, low = split(weight[...])
    depth = weight.shape[0]
    weight_rows[:depth, :] = high
    weight_rows[depth:, :] = high
    weight_low[...] = low
    turned_high, turned_low = split(weight[...].T)
    weight_turned[:, :depth] = turned_high
    weight_turned[:, depth:] = turned_low


def prepare(counts, columns, blocks, weight):
    rows, _, width = blocks.shape
    index = jax.ShapeDtypeStruct(columns.shape, columns.dtype)
    depth, hid = weight.shape
    half = jnp.bfloat16
    return pl.pallas_call(
        functools.partial(prepare_kernel, lax.axis_size("x"), lax.axis_size("core")),
        out_shape=(
            index,
            index,
            jax.ShapeDtypeStruct((rows, 2 * BLK, width), half),
            jax.ShapeDtypeStruct((rows, width, 2 * BLK), half),
            jax.ShapeDtypeStruct((2 * depth, hid), half),
            jax.ShapeDtypeStruct((depth, hid), half),
            jax.ShapeDtypeStruct((hid, 2 * depth), half),
        ),
        in_specs=[pl.BlockSpec(memory_space=pltpu.SMEM)] + vmem(3),
        out_specs=vmem(7),
        compiler_params=params(6),
        cost_estimate=pl.CostEstimate(flops=2_000_000, bytes_accessed=4_000_000, transcendentals=0),
        name="prepare",
    )(counts, columns, blocks, weight)


def layer_kernel(
    places, targets, stacked, turned, p0, p1, p2, p3, p4, p5,
    weight_rows, weight_low, weight_turned, bias, cotangent,
    hidden, sums, other, mine, band, spread, picked, aggregated, grads, sems, out_sems,
):
    pieces = (p0, p1, p2, p3, p4, p5)
    span = p0.shape[0]
    copies = [
        pltpu.make_async_copy(piece, band.at[pl.ds(i * span, span)], sems.at[i])
        for i, piece in enumerate(pieces)
    ]
    for copy in copies:
        copy.start()
    spread[...] = jnp.zeros_like(spread)
    for copy in copies:
        copy.wait()
    rows, _, width = stacked.shape
    slots = width // BLK
    depth = aggregated.shape[1]
    for r in range(rows):
        for k in range(slots):
            start = pl.multiple_of(places[r, k] * BLK, BLK)
            high, low = split(band[pl.ds(start, BLK), :])
            picked[r % 2, k * BLK:(k + 1) * BLK, :depth] = high
            picked[r % 2, k * BLK:(k + 1) * BLK, depth:] = low
        product = dot(stacked[r], picked[r % 2])
        product = product[:BLK] + product[BLK:]
        aggregated[r * BLK:(r + 1) * BLK, :] = product[:, :depth] + product[:, depth:]
    value = aggregated[...]
    high, low = split(value)
    preact = dot(jnp.concatenate([high, low], axis=1), weight_rows[...]) + dot(high, weight_low[...])
    preact = preact + bias[...]
    square = preact * preact
    slope = jnp.tanh(C0 * (preact + C1 * (square * preact)))
    hidden[...] = 0.5 * preact * (1.0 + slope)
    local = 0.5 * (1.0 + slope) + 0.5 * preact * (1.0 - slope * slope) * (C0 * (1.0 + 3.0 * C1 * square))
    dpre = cotangent[...] * local
    dhigh, dlow = split(dpre)
    hid = dpre.shape[1]
    over_rows = ((0,), (0,))
    outer = dot(jnp.concatenate([value, value - high.astype(jnp.float32)], axis=1).T.astype(jnp.bfloat16), dhigh)
    outer = outer[:depth] + outer[depth:] + dot(value.T.astype(jnp.bfloat16), dlow)
    total = jnp.sum(dpre, axis=0, keepdims=True)
    shards = sums.shape[0]
    per = LANES * 2 // shards
    sums[:, :, per * LANES:] = jnp.zeros((shards, 1, LANES), jnp.float32)
    for d in range(shards):
        for j in range(per):
            row = d * per + j
            side, at = row // depth, row % depth
            sums[d, :, j * LANES:(j + 1) * LANES] = outer[at:at + 1, side * LANES:(side + 1) * LANES]
    for side in range(2):
        sums[side, :, per * LANES:] = total[:, side * LANES:(side + 1) * LANES]
    back = dot(jnp.concatenate([dhigh, dlow], axis=0), weight_turned[...])
    count = dpre.shape[0]
    back = back[:count] + back[count:]
    back = back[:, :depth] + back[:, depth:]
    bhigh, blow = split(back)
    for r in range(rows):
        for top in (0, BLK):
            grads[r, top:top + BLK, :depth] = bhigh[r * BLK:(r + 1) * BLK]
            grads[r, top:top + BLK, depth:] = blow[r * BLK:(r + 1) * BLK]
        product = dot(turned[r], grads[r])
        product = product[:, :depth] + product[:, depth:]
        for k in range(slots):
            where = pl.ds(pl.multiple_of(targets[r, k] * BLK, BLK), BLK)
            spread[where, :] = spread[where, :] + product[k * BLK:(k + 1) * BLK]
    half = other.shape[0]
    copies = [
        pltpu.make_async_copy(spread.at[pl.ds(i * half, half)], piece, out_sems.at[i])
        for i, piece in enumerate((other, mine))
    ]
    for copy in copies:
        copy.start()
    for copy in copies:
        copy.wait()


def layer(places, targets, stacked, turned, pieces, weight_rows, weight_low, weight_turned, bias, cotangent, shards):
    rows, _, width = stacked.shape
    span, depth = pieces[0].shape
    count, hid = cotangent.shape
    return pl.pallas_call(
        layer_kernel,
        out_shape=(
            jax.ShapeDtypeStruct((count, hid), jnp.float32),
            jax.ShapeDtypeStruct((shards, 1, depth * hid // shards + LANES), jnp.float32),
            jax.ShapeDtypeStruct((3 * span, depth), jnp.float32),
            jax.ShapeDtypeStruct((3 * span, depth), jnp.float32),
        ),
        in_specs=[pl.BlockSpec(memory_space=pltpu.SMEM)] * 2 + vmem(2)
        + [pl.BlockSpec(memory_space=pl.ANY)] * 6 + vmem(5),
        out_specs=vmem(2) + [pl.BlockSpec(memory_space=pl.ANY)] * 2,
        scratch_shapes=[
            pltpu.VMEM((6 * span, depth), jnp.float32),
            pltpu.VMEM((6 * span, depth), jnp.float32),
            pltpu.VMEM((2, width, 2 * depth), jnp.bfloat16),
            pltpu.VMEM((count, depth), jnp.float32),
            pltpu.VMEM((rows, 2 * BLK, 2 * depth), jnp.bfloat16),
            pltpu.SemaphoreType.DMA((6,)),
            pltpu.SemaphoreType.DMA((2,)),
        ],
        compiler_params=params(14),
        cost_estimate=pl.CostEstimate(flops=700_000_000, bytes_accessed=11_000_000, transcendentals=65536),
        name="layer",
    )(places, targets, stacked, turned, *pieces, weight_rows, weight_low, weight_turned, bias, cotangent)


def sum_kernel(parts, *refs):
    out = refs[-1]
    out[...] = jnp.broadcast_to(jnp.sum(parts[...], axis=0, keepdims=True), out.shape)


def sum_for_all(parts, shards, *behind):
    return pl.pallas_call(
        sum_kernel,
        out_shape=jax.ShapeDtypeStruct((shards,) + parts.shape[1:], parts.dtype),
        in_specs=vmem(1) + [pl.BlockSpec(memory_space=pl.ANY)] * len(behind),
        out_specs=pl.BlockSpec(memory_space=pltpu.VMEM),
        compiler_params=params(4),
        name="sum_for_all",
    )(parts, *behind)


def unpack_kernel(parts, outer, total):
    shards = parts.shape[0]
    depth = outer.shape[0]
    per = LANES * 2 // shards
    for d in range(shards):
        for j in range(per):
            row = d * per + j
            side, at = row // depth, row % depth
            outer[at:at + 1, side * LANES:(side + 1) * LANES] = parts[d, :, j * LANES:(j + 1) * LANES]
    for side in range(2):
        total[:, side * LANES:(side + 1) * LANES] = parts[side, :, per * LANES:]


def unpack(parts, depth, hid):
    return pl.pallas_call(
        unpack_kernel,
        out_shape=(
            jax.ShapeDtypeStruct((depth, hid), jnp.float32),
            jax.ShapeDtypeStruct((1, hid), jnp.float32),
        ),
        in_specs=vmem(1),
        out_specs=vmem(2),
        compiler_params=params(4),
        name="unpack",
    )(parts)


def swap_cores(value):
    return lax.ppermute(value, "core", [(0, 1), (1, 0)])


def along_wide(value, step):
    count = lax.axis_size(WIDE)
    route = [(i, i + step) for i in range(count) if 0 <= i + step < count]
    return lax.ppermute(value, WIDE, route)


def body(features, columns, counts, blocks, weight, bias, cotangent):
    rows, depth = features.shape
    hid = weight.shape[1]
    chips = lax.axis_size("x")
    shards = lax.axis_size(GROUP)
    levels = lax.axis_size("far")
    span = chips * rows

    row_of_chips = jnp.broadcast_to(features[None], (chips, rows, depth))
    own = lax.all_to_all(row_of_chips, "x", 0, 0).reshape(span, depth)
    before = along_wide(own, 1)
    after = along_wide(own, -1)
    own_other = swap_cores(own)
    before_other = swap_cores(before)
    after_other = swap_cores(after)
    places, targets, stacked, turned, weight_rows, weight_low, weight_turned = prepare(
        counts, columns, blocks, weight
    )
    pieces = (before_other, own_other, after_other, before, own, after)
    hidden, sums, to_other, to_mine = layer(
        places, targets, stacked, turned, pieces, weight_rows, weight_low, weight_turned, bias[None], cotangent, shards
    )

    from_core = swap_cores(to_other)
    from_after = along_wide(to_mine[:span] + from_core[:span], -1)
    from_before = along_wide(to_mine[2 * span:] + from_core[2 * span:], 1)
    shares = []
    for step in range(chips):
        chunk = slice(rows * step, rows * (step + 1))
        at = slice(span + rows * step, span + rows * (step + 1))
        share = to_mine[at] + from_core[at] + from_after[chunk] + from_before[chunk]
        if step:
            share = lax.ppermute(share, "x", [(i, (i + step) % chips) for i in range(chips)])
        shares.append(share)
    feature_grad = sum(shares[1:], shares[0])
    scattered = lax.all_to_all(sums, GROUP, 0, 0)
    scattered = lax.all_to_all(sum_for_all(scattered, levels), "far", 0, 0)
    gathered = lax.all_to_all(sum_for_all(scattered, shards, *shares[1:]), GROUP, 0, 0)
    weight_grad, bias_grad = unpack(gathered, depth, hid)

    return (hidden, weight_grad, bias_grad.reshape(hid), feature_grad)


def solution(mesh):
    wide, narrow = mesh.devices.shape
    levels = 32 if wide % 32 == 0 else wide // 2
    fine = Mesh(mesh.devices.reshape(wide // levels, levels // 2, 2, narrow // 2, 2), ALL)
    nodes = P(ALL, None)
    return jax.shard_map(
        body,
        mesh=fine,
        in_specs=(nodes, nodes, P(ALL), P(ALL, None, None), P(), P(), nodes),
        out_specs=(nodes, P(), P(), nodes),
        check_vma=False,
    )
```

```python
import functools
import math

import jax
import jax.numpy as jnp
from jax import lax
from jax.experimental import pallas as pl
from jax.experimental.pallas import tpu as pltpu
from jax.sharding import Mesh, PartitionSpec as P

BLK = 64
LANES = 128
MIB = 1024 * 1024
WIDE = ("y", "far", "near")
ALL = ("y", "far", "near", "x", "core")
GROUP = ("y", "near", "x", "core")
C0 = math.sqrt(2.0 / math.pi)
C1 = 0.044715


def split(value):
    high = value.astype(jnp.bfloat16)
    low = (value - high.astype(jnp.float32)).astype(jnp.bfloat16)
    return high, low


def dot(lhs, rhs, dims=((1,), (0,))):
    return lax.dot_general(lhs, rhs, (dims, ((), ())), preferred_element_type=jnp.float32)


def vmem(count):
    return [pl.BlockSpec(memory_space=pltpu.VMEM)] * count


def params(mib):
    return pltpu.CompilerParams(vmem_limit_bytes=mib * MIB)


def prepare_kernel(
    chips, cores, counts, columns, blocks, weight,
    places, targets, stacked, turned, weight_rows, weight_low, weight_turned,
):
    rows, _, width = blocks.shape
    stripe = rows * chips * cores
    local = columns[...] - (lax.axis_index(WIDE) - 1) * stripe
    part = local >> (stripe.bit_length() - 1)
    block = local & (rows - 1)
    device = (local & (stripe - 1)) >> (rows.bit_length() - 1)
    chip = device >> (cores.bit_length() - 1)
    mine = ((device ^ lax.axis_index("core")) & (cores - 1)) ^ 1
    band = mine * 3 + part
    ahead = (chip - lax.axis_index("x")) & (chips - 1)
    places[...] = (band * chips + chip) * rows + block
    targets[...] = (band * chips + ahead) * rows + block
    slot = lax.broadcasted_iota(jnp.int32, (BLK, width), 1) // BLK
    for r in range(rows):
        masked = jnp.where(slot < counts[r], blocks[r], 0.0)
        high, low = split(masked)
        stacked[r, :BLK, :] = high
        stacked[r, BLK:, :] = low
        both = jnp.concatenate([masked, masked - high.astype(jnp.float32)], axis=0)
        turned[r] = both.T.astype(jnp.bfloat16)
    high, low = split(weight[...])
    depth = weight.shape[0]
    weight_rows[:depth, :] = high
    weight_rows[depth:, :] = high
    weight_low[...] = low
    turned_high, turned_low = split(weight[...].T)
    weight_turned[:, :depth] = turned_high
    weight_turned[:, depth:] = turned_low


def prepare(counts, columns, blocks, weight):
    rows, _, width = blocks.shape
    index = jax.ShapeDtypeStruct(columns.shape, columns.dtype)
    depth, hid = weight.shape
    half = jnp.bfloat16
    return pl.pallas_call(
        functools.partial(prepare_kernel, lax.axis_size("x"), lax.axis_size("core")),
        out_shape=(
            index,
            index,
            jax.ShapeDtypeStruct((rows, 2 * BLK, width), half),
            jax.ShapeDtypeStruct((rows, width, 2 * BLK), half),
            jax.ShapeDtypeStruct((2 * depth, hid), half),
            jax.ShapeDtypeStruct((depth, hid), half),
            jax.ShapeDtypeStruct((hid, 2 * depth), half),
        ),
        in_specs=[pl.BlockSpec(memory_space=pltpu.SMEM)] + vmem(3),
        out_specs=vmem(7),
        compiler_params=params(6),
        cost_estimate=pl.CostEstimate(flops=2_000_000, bytes_accessed=4_000_000, transcendentals=0),
        name="prepare",
    )(counts, columns, blocks, weight)


def layer_kernel(
    places, targets, stacked, turned, p0, p1, p2, p3, p4, p5,
    weight_rows, weight_low, weight_turned, bias, cotangent,
    hidden, sums, other, mine, band, spread, picked, aggregated, grads, sems, out_sems,
):
    pieces = (p0, p1, p2, p3, p4, p5)
    span = p0.shape[0]
    copies = [
        pltpu.make_async_copy(piece, band.at[pl.ds(i * span, span)], sems.at[i])
        for i, piece in enumerate(pieces)
    ]
    for copy in copies:
        copy.start()
    spread[...] = jnp.zeros_like(spread)
    for copy in copies:
        copy.wait()
    rows, _, width = stacked.shape
    slots = width // BLK
    depth = aggregated.shape[1]
    for r in range(rows):
        for k in range(slots):
            start = pl.multiple_of(places[r, k] * BLK, BLK)
            high, low = split(band[pl.ds(start, BLK), :])
            picked[r, k * BLK:(k + 1) * BLK, :depth] = high
            picked[r, k * BLK:(k + 1) * BLK, depth:] = low
        product = dot(stacked[r], picked[r])
        product = product[:BLK] + product[BLK:]
        aggregated[r * BLK:(r + 1) * BLK, :] = product[:, :depth] + product[:, depth:]
    value = aggregated[...]
    high, low = split(value)
    preact = dot(jnp.concatenate([high, low], axis=1), weight_rows[...]) + dot(high, weight_low[...])
    preact = preact + bias[...]
    square = preact * preact
    slope = jnp.tanh(C0 * (preact + C1 * (square * preact)))
    hidden[...] = 0.5 * preact * (1.0 + slope)
    local = 0.5 * (1.0 + slope) + 0.5 * preact * (1.0 - slope * slope) * (C0 * (1.0 + 3.0 * C1 * square))
    dpre = cotangent[...] * local
    dhigh, dlow = split(dpre)
    hid = dpre.shape[1]
    over_rows = ((0,), (0,))
    outer = dot(jnp.concatenate([value, value - high.astype(jnp.float32)], axis=1).T.astype(jnp.bfloat16), dhigh)
    outer = outer[:depth] + outer[depth:] + dot(value.T.astype(jnp.bfloat16), dlow)
    total = jnp.sum(dpre, axis=0, keepdims=True)
    shards = sums.shape[0]
    per = LANES * 2 // shards
    sums[:, :, per * LANES:] = jnp.zeros((shards, 1, LANES), jnp.float32)
    for d in range(shards):
        for j in range(per):
            row = d * per + j
            side, at = row // depth, row % depth
            sums[d, :, j * LANES:(j + 1) * LANES] = outer[at:at + 1, side * LANES:(side + 1) * LANES]
    for side in range(2):
        sums[side, :, per * LANES:] = total[:, side * LANES:(side + 1) * LANES]
    back = dot(jnp.concatenate([dhigh, dlow], axis=0), weight_turned[...])
    count = dpre.shape[0]
    back = back[:count] + back[count:]
    back = back[:, :depth] + back[:, depth:]
    bhigh, blow = split(back)
    for r in range(rows):
        for top in (0, BLK):
            grads[r, top:top + BLK, :depth] = bhigh[r * BLK:(r + 1) * BLK]
            grads[r, top:top + BLK, depth:] = blow[r * BLK:(r + 1) * BLK]
        product = dot(turned[r], grads[r])
        product = product[:, :depth] + product[:, depth:]
        for k in range(slots):
            where = pl.ds(pl.multiple_of(targets[r, k] * BLK, BLK), BLK)
            spread[where, :] = spread[where, :] + product[k * BLK:(k + 1) * BLK]
    half = other.shape[0]
    copies = [
        pltpu.make_async_copy(spread.at[pl.ds(i * half, half)], piece, out_sems.at[i])
        for i, piece in enumerate((other, mine))
    ]
    for copy in copies:
        copy.start()
    for copy in copies:
        copy.wait()


def layer(places, targets, stacked, turned, pieces, weight_rows, weight_low, weight_turned, bias, cotangent, shards):
    rows, _, width = stacked.shape
    span, depth = pieces[0].shape
    count, hid = cotangent.shape
    return pl.pallas_call(
        layer_kernel,
        out_shape=(
            jax.ShapeDtypeStruct((count, hid), jnp.float32),
            jax.ShapeDtypeStruct((shards, 1, depth * hid // shards + LANES), jnp.float32),
            jax.ShapeDtypeStruct((3 * span, depth), jnp.float32),
            jax.ShapeDtypeStruct((3 * span, depth), jnp.float32),
        ),
        in_specs=[pl.BlockSpec(memory_space=pltpu.SMEM)] * 2 + vmem(2)
        + [pl.BlockSpec(memory_space=pl.ANY)] * 6 + vmem(5),
        out_specs=vmem(2) + [pl.BlockSpec(memory_space=pl.ANY)] * 2,
        scratch_shapes=[
            pltpu.VMEM((6 * span, depth), jnp.float32),
            pltpu.VMEM((6 * span, depth), jnp.float32),
            pltpu.VMEM((rows, width, 2 * depth), jnp.bfloat16),
            pltpu.VMEM((count, depth), jnp.float32),
            pltpu.VMEM((rows, 2 * BLK, 2 * depth), jnp.bfloat16),
            pltpu.SemaphoreType.DMA((6,)),
            pltpu.SemaphoreType.DMA((2,)),
        ],
        compiler_params=params(15),
        cost_estimate=pl.CostEstimate(flops=700_000_000, bytes_accessed=11_000_000, transcendentals=65536),
        name="layer",
    )(places, targets, stacked, turned, *pieces, weight_rows, weight_low, weight_turned, bias, cotangent)


def sum_kernel(parts, *refs):
    out = refs[-1]
    out[...] = jnp.broadcast_to(jnp.sum(parts[...], axis=0, keepdims=True), out.shape)


def sum_for_all(parts, shards, *behind):
    return pl.pallas_call(
        sum_kernel,
        out_shape=jax.ShapeDtypeStruct((shards,) + parts.shape[1:], parts.dtype),
        in_specs=vmem(1) + [pl.BlockSpec(memory_space=pl.ANY)] * len(behind),
        out_specs=pl.BlockSpec(memory_space=pltpu.VMEM),
        compiler_params=params(4),
        name="sum_for_all",
    )(parts, *behind)


def unpack_kernel(parts, outer, total):
    shards = parts.shape[0]
    depth = outer.shape[0]
    per = LANES * 2 // shards
    for d in range(shards):
        for j in range(per):
            row = d * per + j
            side, at = row // depth, row % depth
            outer[at:at + 1, side * LANES:(side + 1) * LANES] = parts[d, :, j * LANES:(j + 1) * LANES]
    for side in range(2):
        total[:, side * LANES:(side + 1) * LANES] = parts[side, :, per * LANES:]


def unpack(parts, depth, hid):
    return pl.pallas_call(
        unpack_kernel,
        out_shape=(
            jax.ShapeDtypeStruct((depth, hid), jnp.float32),
            jax.ShapeDtypeStruct((1, hid), jnp.float32),
        ),
        in_specs=vmem(1),
        out_specs=vmem(2),
        compiler_params=params(4),
        name="unpack",
    )(parts)


def swap_cores(value):
    return lax.ppermute(value, "core", [(0, 1), (1, 0)])


def along_wide(value, step):
    count = lax.axis_size(WIDE)
    route = [(i, i + step) for i in range(count) if 0 <= i + step < count]
    return lax.ppermute(value, WIDE, route)


def body(features, columns, counts, blocks, weight, bias, cotangent):
    rows, depth = features.shape
    hid = weight.shape[1]
    chips = lax.axis_size("x")
    shards = lax.axis_size(GROUP)
    levels = lax.axis_size("far")
    span = chips * rows

    own = lax.all_gather(features, "x", axis=0, tiled=True)
    before = along_wide(own, 1)
    after = along_wide(own, -1)
    own_other = swap_cores(own)
    before_other = swap_cores(before)
    after_other = swap_cores(after)
    places, targets, stacked, turned, weight_rows, weight_low, weight_turned = prepare(
        counts, columns, blocks, weight
    )
    pieces = (before_other, own_other, after_other, before, own, after)
    hidden, sums, to_other, to_mine = layer(
        places, targets, stacked, turned, pieces, weight_rows, weight_low, weight_turned, bias[None], cotangent, shards
    )

    from_core = swap_cores(to_other)
    from_after = along_wide(to_mine[:span] + from_core[:span], -1)
    from_before = along_wide(to_mine[2 * span:] + from_core[2 * span:], 1)
    shares = []
    for step in range(chips):
        chunk = slice(rows * step, rows * (step + 1))
        at = slice(span + rows * step, span + rows * (step + 1))
        share = to_mine[at] + from_core[at] + from_after[chunk] + from_before[chunk]
        if step:
            share = lax.ppermute(share, "x", [(i, (i + step) % chips) for i in range(chips)])
        shares.append(share)
    feature_grad = sum(shares[1:], shares[0])
    scattered = lax.all_to_all(sums, GROUP, 0, 0)
    scattered = lax.all_to_all(sum_for_all(scattered, levels), "far", 0, 0)
    gathered = lax.all_to_all(sum_for_all(scattered, shards, *shares[1:]), GROUP, 0, 0)
    weight_grad, bias_grad = unpack(gathered, depth, hid)

    return (hidden, weight_grad, bias_grad.reshape(hid), feature_grad)


def solution(mesh):
    wide, narrow = mesh.devices.shape
    levels = 32 if wide % 32 == 0 else wide // 2
    fine = Mesh(mesh.devices.reshape(wide // levels, levels // 2, 2, narrow // 2, 2), ALL)
    nodes = P(ALL, None)
    return jax.shard_map(
        body,
        mesh=fine,
        in_specs=(nodes, nodes, P(ALL), P(ALL, None, None), P(), P(), nodes),
        out_specs=(nodes, P(), P(), nodes),
        check_vma=False,
    )
```
